256 devices in a mesh: seq: 64 (over x, z, core), tp: 4 (over y).
Axes of the slice: x: 4, y: 4, z: 8, core: 2. Of those that a mesh axis runs over, the one named last changes fastest.
Arguments:
- picked: int32 [4096], P('seq'), may hold values from -1 to 16383, as said below
- owner_perm: int32 [64], replicated, may hold values from 0 to 63, each once
- router_logit: bfloat16 [16384], P('seq'), may hold values from -6 to 6
- queries: bfloat16 [4096, 3072], P('seq', 'tp'), may hold values from -6.5 to 6.5
- keys: bfloat16 [4096, 3072], P('seq', 'tp'), may hold values from -6.5 to 6.5
- values: bfloat16 [4096, 3072], P('seq', 'tp'), may hold values from -6 to 6
- out_grad: bfloat16 [2048, 3072], P('seq', 'tp'), may hold values from -6 to 6
Outputs:
- gated_out: bfloat16 [2048, 3072], P('seq', 'tp')
- query_grad: bfloat16 [4096, 3072], P('seq', 'tp')
- key_grad: bfloat16 [4096, 3072], P('seq', 'tp')
- value_grad: bfloat16 [4096, 3072], P('seq', 'tp')
- router_grad: float32 [16384], P('seq')
The draws below stay inside these ranges and needn't reach their ends.
Inputs may be any that keep to these rules, and one draw needn't show every extreme that they name: Block h lists, in increasing order, the picked positions of shard h (from h * 256 to (h + 1) * 256 - 1), then -1 in its unused entries. All blocks together list exactly 2048 positions, and some block is full.
All inputs are finite; a program needn't handle non-finite values.
Results may differ from the reference program's by a relative error of at most 0.04.
Values may be sent and summed in bfloat16 or wider, within the bound.
A program may use at most 128 MiB of HBM per device.

```python
import jax
import jax.numpy as jnp
from jax import lax

HEADS = 24
HD = 128
TOK_DEV = 256
PICK = 32
CAP = 64
TOKENS = 16384
PICKED = 2048
SLOTS = 4096
FEAT = 3072
N_SEQ = 64


def draw_queries(key, part):
    key = jax.random.fold_in(key, 7)
    drawn = jnp.clip(1.7 * jax.random.normal(key, (SLOTS, FEAT), jnp.float32), -6.5, 6.5)
    return drawn.astype(jnp.bfloat16)


def draw_keys(key, part):
    key = jax.random.fold_in(key, 8)
    drawn = jnp.clip(1.7 * jax.random.normal(key, (SLOTS, FEAT), jnp.float32), -6.5, 6.5)
    return drawn.astype(jnp.bfloat16)


def draw_picked(key, part):
    key = jax.random.fold_in(key, 3)
    pairing = jax.random.permutation(jax.random.fold_in(key, 1), N_SEQ)
    shifts = jax.random.randint(jax.random.fold_in(key, 2), (N_SEQ // 2,), 0, PICK + 1)
    shifts = shifts.at[0].set(PICK)
    signed = jnp.stack([shifts, -shifts], axis=1).reshape(-1)
    counts = jnp.zeros((N_SEQ,), jnp.int32).at[pairing].set((PICK + signed).astype(jnp.int32))
    column = jnp.arange(TOK_DEV, dtype=jnp.int32)
    scores = jax.random.randint(jax.random.fold_in(key, 4), (N_SEQ, TOK_DEV), 0, 65536) * TOK_DEV + column[None, :]
    ranking = jnp.argsort(jnp.argsort(scores, axis=1), axis=1)
    chosen = ranking < counts[:, None]
    sorting = jnp.where(chosen, column[None, :], TOK_DEV + column[None, :])
    ordered = jnp.sort(sorting, axis=1)[:, :CAP]
    shard_base = (jnp.arange(N_SEQ, dtype=jnp.int32) * TOK_DEV)[:, None]
    return jnp.where(ordered < TOK_DEV, ordered + shard_base, -1).reshape(-1).astype(jnp.int32)


def steps_of(stream_key, dims, split, low, largest):
    gain = 1.0
    for axis_at, blocks in split:
        steps = jax.random.uniform(jax.random.fold_in(jax.random.fold_in(stream_key, 6), axis_at), (blocks,), jnp.float32, low / len(split), largest / len(split))
        gain = gain * jnp.repeat(jnp.exp(steps), dims[axis_at] // blocks).reshape((-1,) + (1,) * (len(dims) - 1 - axis_at))
    return gain


def normal_values(stream_key, shape, width, limit, pieces=(), held_as=jnp.bfloat16):
    gain = steps_of(stream_key, shape, pieces, -0.22, 0.18) if pieces else 1.0
    array = jax.random.normal(stream_key, shape, jnp.float32) * width * gain
    return jnp.minimum(jnp.maximum(array, -limit), limit).astype(held_as)


def setup_inputs(seed: int = 0) -> dict:
    arg_keys = jax.random.split(jax.random.key(seed), 8)
    picked = draw_picked(jax.random.fold_in(arg_keys[7], 71), 0)
    owner_perm = jax.random.permutation(arg_keys[1], N_SEQ).astype(jnp.int32)
    router_logit = normal_values(arg_keys[2], (TOKENS,), 2.0, 6.0, ((0, 64),))
    queries = draw_queries(jax.random.fold_in(arg_keys[7], 71), 0)
    keys = draw_keys(jax.random.fold_in(arg_keys[7], 71), 0)
    values = normal_values(arg_keys[5], (SLOTS, FEAT), 1.0, 6.0, ((0, 64), (1, 4)))
    out_grad = normal_values(arg_keys[6], (PICKED, FEAT), 1.0, 6.0, ((0, 64), (1, 4)))
    return {"picked": picked, "owner_perm": owner_perm, "router_logit": router_logit, "queries": queries, "keys": keys, "values": values, "out_grad": out_grad}


NEG_FILL = -1.0e30


def reference(picked, owner_perm, router_logit, queries, keys, values, out_grad):
    blocks = picked.reshape(N_SEQ, CAP)
    counts = jnp.sum((blocks >= 0).astype(jnp.int32), axis=1).astype(jnp.int32)
    ends_at = jnp.cumsum(counts).astype(jnp.int32)
    starts_at = ends_at - counts
    order_ids = jnp.arange(PICKED, dtype=jnp.int32)
    home_of = jnp.sum((ends_at[None, :] <= order_ids[:, None]).astype(jnp.int32), axis=1).astype(jnp.int32)
    source = (home_of * CAP + order_ids - starts_at[home_of]).astype(jnp.int32)
    position = picked[source]
    query_all = queries[source]
    key_all = keys[source]
    value_all = values[source]
    gate_value = jax.nn.sigmoid(router_logit[position].astype(jnp.float32))
    owner_row = (owner_perm[order_ids % N_SEQ] * PICK + order_ids // N_SEQ).astype(jnp.int32)
    grad_rows = out_grad[owner_row]
    allowed = order_ids[None, :] <= order_ids[:, None]
    scale_factor = HD ** -0.5
    head_ids = jnp.arange(HEADS, dtype=jnp.int32)

    def head_scores(head_id):
        query_head = lax.dynamic_slice_in_dim(query_all, head_id * HD, HD, 1)
        key_head = lax.dynamic_slice_in_dim(key_all, head_id * HD, HD, 1)
        scores = jnp.dot(query_head, key_head.T, preferred_element_type=jnp.float32) * scale_factor
        return query_head, key_head, jnp.where(allowed, scores, NEG_FILL)

    def forward_head(head_id):
        query_head, key_head, masked = head_scores(head_id)
        value_head = lax.dynamic_slice_in_dim(value_all, head_id * HD, HD, 1)
        row_top = jnp.max(masked, axis=1)
        log_total = row_top + jnp.log(jnp.sum(jnp.exp(masked - row_top[:, None]), axis=1))
        weights = jnp.where(allowed, jnp.exp(masked - log_total[:, None]), 0.0)
        attended = jnp.dot(weights.astype(jnp.bfloat16), value_head, preferred_element_type=jnp.float32)
        return attended, log_total

    attended, log_total = lax.map(forward_head, head_ids)
    attended_rows = jnp.transpose(attended, (1, 0, 2)).reshape(PICKED, FEAT)
    gated = (gate_value[:, None] * attended_rows).astype(jnp.bfloat16)
    gated_out = jnp.zeros((PICKED, FEAT), jnp.bfloat16).at[owner_row].set(gated)
    gate_grad = jnp.sum(grad_rows.astype(jnp.float32) * attended_rows, axis=1)
    logit_grad = gate_grad * gate_value * (1.0 - gate_value)
    router_grad = jnp.zeros((TOKENS,), jnp.float32).at[position].set(logit_grad)
    out_rounded = (gate_value[:, None] * grad_rows.astype(jnp.float32)).astype(jnp.bfloat16)
    row_delta = jnp.sum((out_rounded.astype(jnp.float32) * attended_rows).reshape(PICKED, HEADS, HD), axis=2)

    def backward_head(head_id):
        query_head, key_head, masked = head_scores(head_id)
        value_head = lax.dynamic_slice_in_dim(value_all, head_id * HD, HD, 1)
        grad_head = lax.dynamic_slice_in_dim(out_rounded, head_id * HD, HD, 1)
        total_head = log_total[head_id]
        delta_head = row_delta[:, head_id]
        weights = jnp.where(allowed, jnp.exp(masked - total_head[:, None]), 0.0)
        value_grad = jnp.dot(weights.astype(jnp.bfloat16).T, grad_head, preferred_element_type=jnp.float32)
        prob_grad = jnp.dot(grad_head, value_head.T, preferred_element_type=jnp.float32)
        score_grad = (weights * (prob_grad - delta_head[:, None])).astype(jnp.bfloat16)
        query_grad = jnp.dot(score_grad, key_head, preferred_element_type=jnp.float32) * scale_factor
        key_grad = jnp.dot(score_grad.T, query_head, preferred_element_type=jnp.float32) * scale_factor
        return query_grad, key_grad, value_grad

    query_heads, key_heads, value_heads = lax.map(backward_head, head_ids)

    def to_home(stacked):
        flat_rows = jnp.transpose(stacked, (1, 0, 2)).reshape(PICKED, FEAT).astype(jnp.bfloat16)
        return jnp.zeros((SLOTS, FEAT), jnp.bfloat16).at[source].set(flat_rows)

    return gated_out, to_home(query_heads), to_home(key_heads), to_home(value_heads), router_grad
```

```python
import functools

import jax
import jax.numpy as jnp
from jax import lax
from jax.experimental import pallas as pl
from jax.experimental.pallas import tpu as pltpu
from jax.sharding import PartitionSpec as P

HD = 128
SEQ = 64
CAP = 64
TOK = 256
WPH = 8
CLS = 256
MSG = 16
SCALE = HD ** -0.5
MESH = pl.DeviceIdType.MESH
BF16, F32, I32 = jnp.bfloat16, jnp.float32, jnp.int32


def iota(shape, axis):
    return lax.broadcasted_iota(I32, shape, axis)


def onehot(hit):
    return jnp.where(hit, 1.0, 0.0).astype(BF16)


def dot(a, b):
    return lax.dot_general(a, b, (((1,), (0,)), ((), ())), preferred_element_type=F32)


def dot_nt(a, b):
    return lax.dot_general(a, b, (((1,), (1,)), ((), ())), preferred_element_type=F32)


def dot_tn(a, b):
    return lax.dot_general(a, b, (((0,), (0,)), ((), ())), preferred_element_type=F32)


def place_of(head, cls):
    z = head + head // 3
    return (cls // 2) * 16 + z * 2 + lax.rem(cls, 2)


def remote(src, dst, send, recv, device):
    return pltpu.make_async_remote_copy(
        src_ref=src, dst_ref=dst, send_sem=send, recv_sem=recv, device_id=device, device_id_type=MESH
    )


def kernel(
    n_tp,
    heads,
    picked_ref,
    perm_ref,
    logit_ref,
    q_ref,
    k_ref,
    v_ref,
    d_ref,
    gated_ref,
    dq_ref,
    dk_ref,
    dv_ref,
    router_ref,
    cnt_out,
    cnt,
    msg,
    rows,
    own,
    kv,
    dsend,
    dcls,
    sbuf,
    pbuf,
    part,
    psum,
    gsend,
    gchk,
    gg,
    back,
    home,
    send_sem,
    recv_sem,
    kv_sem,
    ps_sem,
    loc_sem,
):
    me = lax.axis_index("seq")
    tp = lax.axis_index("tp")
    z = lax.rem(lax.div(me, 2), 8)
    core = lax.rem(me, 2)
    x = lax.div(me, 16)
    is_worker = lax.rem(z, 4) < 3
    head = z - lax.div(z, 4)
    cls = x * 2 + core
    slot = head * WPH + cls
    workers = heads * WPH

    barrier = pltpu.get_barrier_semaphore()

    def greet(n, carry):
        pl.semaphore_signal(barrier, inc=1, device_id={"seq": lax.rem(me + n, SEQ)}, device_id_type=MESH)
        return carry

    lax.fori_loop(1, SEQ, greet, 0)
    for n in range(1, n_tp):
        pl.semaphore_signal(barrier, inc=1, device_id={"tp": lax.rem(tp + n, n_tp)}, device_id_type=MESH)

    picked = picked_ref[...]
    count = jnp.sum(jnp.where(picked >= 0, 1, 0), axis=1, keepdims=True)
    cnt_out[...] = jnp.broadcast_to(count, (1, 128))
    pl.semaphore_wait(barrier, SEQ - 1 + n_tp - 1)

    def send_count(n, carry):
        remote(cnt_out, cnt.at[me], send_sem.at[0], recv_sem.at[0], {"seq": lax.rem(me + n, SEQ)}).start()
        return carry

    lax.fori_loop(1, SEQ, send_count, 0)
    cnt[me] = cnt_out[...]

    eye = iota((CAP, CAP), 0) == iota((CAP, CAP), 1)
    picked_col = jnp.sum(jnp.where(eye, jnp.broadcast_to(picked, (CAP, CAP)), 0), axis=1, keepdims=True)
    spots = jnp.broadcast_to(picked_col - me * TOK, (CAP, TOK)) == iota((CAP, TOK), 1)
    logits = jnp.broadcast_to(logit_ref[...].astype(F32), (CAP, TOK))
    logit_col = jnp.sum(jnp.where(spots, logits, 0.0), axis=1, keepdims=True)
    gate_col = 1.0 / (1.0 + jnp.exp(-logit_col))
    spread = jnp.where(iota((CAP, 128), 1) == (iota((CAP, 128), 0) >> 3), jnp.broadcast_to(logit_col, (CAP, 128)), 0.0)
    spread = spread.astype(BF16)

    remote(cnt.at[pl.ds(0, SEQ - 1)], cnt.at[pl.ds(0, SEQ - 1)], send_sem.at[0], recv_sem.at[0], {"seq": me}).wait_recv()
    counts = jnp.sum(cnt[...], axis=1)
    start = jnp.sum(jnp.where(iota((SEQ, 128), 0) < me, counts, 0), axis=0, keepdims=True)

    n_out = iota((WPH * MSG, 128), 0)
    t_out = n_out & 15
    turn = ((n_out >> 4) - start) & 7
    src = iota((WPH * MSG, 128), 1)
    pick_left = onehot(src == 8 * t_out + turn)
    right_at = jnp.where(t_out < 8, 8 * t_out + turn, jnp.where(t_out < 12, CAP + 4 * (n_out >> 4) + t_out - 8, -1))
    pick_right = onehot(src == right_at)
    src64 = iota((WPH * MSG, CAP), 1)
    pick_logit = onehot((t_out[:, :CAP] == 12) & ((src64 & 7) == turn[:, :CAP]))
    logit_rows = dot(pick_logit, spread)
    for k in range(heads):
        cols = slice(k * HD, (k + 1) * HD)
        left = dot(pick_left, jnp.concatenate([q_ref[:, cols], k_ref[:, cols]], axis=0))
        fill = jnp.zeros((32, HD), BF16)
        right = dot(pick_right, jnp.concatenate([v_ref[:, cols], d_ref[:, cols], fill], axis=0)) + logit_rows
        both = jnp.concatenate([left, right], axis=1).astype(BF16)
        msg[pl.ds(k * WPH, WPH)] = both.reshape(WPH, MSG, 2 * HD)

    def send_rows(n, carry):
        w = lax.rem(n + me, workers)
        dst = place_of(lax.div(w, WPH), lax.rem(w, WPH))

        @pl.when(dst != me)
        def _():
            remote(msg.at[w], rows.at[me], send_sem.at[1], recv_sem.at[1], {"seq": dst}).start()

        return carry

    lax.fori_loop(0, workers, send_rows, 0)

    @pl.when(is_worker)
    def _():
        own_rows = pltpu.make_async_copy(msg.at[slot], rows.at[me], loc_sem.at[0])
        own_rows.start()

        n_row = iota((SEQ, SEQ * MSG), 1)
        below = jnp.concatenate([counts] * 8, axis=1)
        at_h = iota((SEQ, SEQ * MSG), 0)
        start_n = jnp.sum(jnp.where(at_h < (n_row >> 4), below, 0), axis=0, keepdims=True)
        end_n = jnp.sum(jnp.where(at_h <= (n_row >> 4), below, 0), axis=0, keepdims=True)
        t_n = iota((1, SEQ * MSG), 1) & 15
        p_n = ((start_n - cls + 7) >> 3) + (t_n & 7)
        live_n = p_n < ((end_n - cls + 7) >> 3)
        q_at = jnp.where(live_n & (t_n < 8), p_n, -1)
        k_at = jnp.where(live_n & (t_n >= 8), p_n, -1)
        p_sub = iota((CLS, SEQ * MSG), 0)
        take_q = onehot(p_sub == q_at)
        take_k = onehot(p_sub == k_at)
        m_sub = iota((CLS, SEQ), 0)
        residue_m = 8 * (m_sub & 7) + (m_sub >> 5)
        perm = jnp.broadcast_to(perm_ref[...], (CLS, SEQ))
        owner_m = jnp.sum(jnp.where(iota((CLS, SEQ), 1) == residue_m, perm, 0), axis=1, keepdims=True)
        d_at = MSG * owner_m + 8 + ((iota((CLS, 1), 0) & 31) >> 3)
        take_d = onehot(iota((CLS, SEQ * MSG), 1) == d_at)
        take_l = onehot(n_row == MSG * at_h + 12)

        tri = onehot(iota((SEQ, SEQ), 1) < iota((SEQ, SEQ), 0))
        starts = dot(tri, counts.astype(BF16)).astype(I32)
        base = (starts - cls + 7) >> 3
        after = (starts + counts - cls + 7) >> 3
        base2 = jnp.concatenate([base, base], axis=1)
        after2 = jnp.concatenate([after, after], axis=1)
        p_lane = iota((SEQ, CLS), 1)
        of_home = (base2 <= p_lane) & (p_lane < after2)
        lane_p = jnp.sum(jnp.where(of_home, p_lane - base2, 0), axis=0, keepdims=True)
        lanes = onehot(iota((128, CLS), 0) == lane_p)

        remote(rows.at[pl.ds(0, SEQ - 1)], rows.at[pl.ds(0, SEQ - 1)], send_sem.at[1], recv_sem.at[1], {"seq": me}).wait_recv()
        own_rows.wait()
        got = rows[...].reshape(SEQ * MSG, 2 * HD)
        qv = dot(take_q, got).astype(BF16)
        kc = dot(take_k, got[:, :HD]).astype(BF16)
        own[0] = qv[:, :HD]
        kv[cls] = jnp.concatenate([kc, qv[:, HD:]], axis=1)
        dsend[...] = dot(take_d, got[:, HD:]).astype(BF16).reshape(WPH, 32, HD)

        def send_kv(n, carry):
            to = lax.rem(cls + n, WPH)
            dst = {"seq": place_of(head, to)}
            remote(kv.at[cls], kv.at[cls], send_sem.at[2], kv_sem.at[cls], dst).start()
            remote(dsend.at[to], dcls.at[cls], send_sem.at[3], recv_sem.at[2], dst).start()
            return carry

        lax.fori_loop(1, WPH, send_kv, 0)
        dcls[cls] = dsend[cls]

        logit_h = dot(take_l, got[:, HD:]).astype(BF16)
        logit_p = jnp.sum(jnp.where(of_home, dot(logit_h, lanes), 0.0), axis=0, keepdims=True)
        gate = 1.0 / (1.0 + jnp.exp(-logit_p))

        q = own[0]
        top = jnp.full((1, CLS), -jnp.inf, F32)
        k_sub, q_lane = iota((CLS, CLS), 0), iota((CLS, CLS), 1)
        for n in range(WPH):
            other = lax.rem(cls + n, WPH)
            if n:
                remote(kv.at[other], kv.at[other], send_sem.at[2], kv_sem.at[other], {"seq": me}).wait_recv()
            later = jnp.where(other > cls, 1, 0)
            s = dot_nt(kv[other, :, :HD], q) * SCALE
            s = jnp.where(k_sub + later <= q_lane, s, -1e30)
            sbuf[n] = s
            top = jnp.maximum(top, jnp.max(s, axis=0, keepdims=True))
        total = jnp.zeros((1, CLS), F32)
        for n in range(WPH):
            e = jnp.exp(sbuf[n] - top)
            sbuf[n] = e
            total = total + jnp.sum(e, axis=0, keepdims=True)
        inv = 1.0 / total
        out_t = jnp.zeros((HD, CLS), F32)
        for n in range(WPH):
            other = lax.rem(cls + n, WPH)
            w = sbuf[n] * inv
            sbuf[n] = w
            wb = w.astype(BF16)
            pbuf[n] = wb
            out_t = out_t + dot_tn(kv[other, :, HD:], wb)

        remote(dcls.at[pl.ds(0, WPH - 1)], dcls.at[pl.ds(0, WPH - 1)], send_sem.at[3], recv_sem.at[2], {"seq": me}).wait_recv()
        dy_t = dcls[...].reshape(CLS, HD).astype(F32).T
        dor_t = (dy_t * gate).astype(BF16).astype(F32)
        dor = dor_t.T.astype(BF16)
        delta = jnp.sum(dor_t * out_t, axis=0, keepdims=True)
        gate_grad = jnp.sum(dy_t * out_t, axis=0, keepdims=True)
        gsend[...] = (out_t * gate).T.astype(BF16).reshape(WPH, 32, HD)
        gg[tp] = jnp.broadcast_to(gate_grad, (8, CLS))

        def send_gated(n, carry):
            to = lax.rem(cls + n, WPH)
            remote(gsend.at[to], gchk.at[cls], send_sem.at[4], recv_sem.at[3], {"seq": place_of(head, to)}).start()
            return carry

        lax.fori_loop(1, WPH, send_gated, 0)
        gchk[cls] = gsend[cls]
        for n in range(1, n_tp):
            remote(gg.at[tp], gg.at[tp], send_sem.at[5], recv_sem.at[4], {"tp": lax.rem(tp + n, n_tp)}).start()

        dq_t = jnp.zeros((HD, CLS), F32)
        mine = None
        for n in list(range(1, WPH)) + [0]:
            other = lax.rem(cls + n, WPH)
            dp = dot_nt(kv[other, :, HD:], dor)
            ds = (sbuf[n] * (dp - delta)).astype(BF16)
            dq_t = dq_t + dot_tn(kv[other, :, :HD], ds)
            grads = jnp.concatenate([dot(ds, q) * SCALE, dot(pbuf[n], dor)], axis=1)
            if n:
                part[n] = grads.astype(BF16)
                remote(part.at[n], psum.at[cls], send_sem.at[6], ps_sem.at[cls], {"seq": place_of(head, other)}).start()
            else:
                mine = grads
        dqc = (dq_t * SCALE).T.astype(BF16)

        n_sub = iota((SEQ * MSG, SEQ), 0)
        rep = onehot((n_sub >> 4) == iota((SEQ * MSG, SEQ), 1))
        perm_o = jnp.broadcast_to(perm_ref[...], (SEQ, SEQ))
        res_o = jnp.sum(jnp.where(perm_o == iota((SEQ, SEQ), 0), iota((SEQ, SEQ), 1), 0), axis=1, keepdims=True)
        three = jnp.concatenate([base, after, jnp.broadcast_to(res_o, (SEQ, 128))], axis=1).astype(F32).astype(BF16)
        wide = dot(rep, three).astype(I32)
        t_col = iota((SEQ * MSG, 128), 0) & 15
        p_col = wide[:, :128] + (t_col & 7)
        live_col = p_col < wide[:, 128:256]
        res_col = wide[:, 256:]
        q_to = jnp.where(live_col & (t_col < 8), p_col, -1)
        k_to = jnp.where(live_col & (t_col >= 8), p_col, -1)
        o_to = jnp.where((t_col >= 8) & (t_col < 12), 32 * (res_col & 7) + 8 * (t_col - 8) + (res_col >> 3), -1)
        p_at = iota((SEQ * MSG, CLS), 1)
        put_q = onehot(p_at == jnp.concatenate([q_to, q_to], axis=1))
        put_k = onehot(p_at == jnp.concatenate([k_to, k_to], axis=1))
        put_o = onehot(p_at == jnp.concatenate([o_to, o_to], axis=1))
        put_g = onehot(iota((SEQ * MSG, SEQ), 0) == MSG * iota((SEQ * MSG, SEQ), 1) + 12)

        if n_tp > 1:
            others = gg.at[pl.ds(0, n_tp - 1)]
            remote(others, others, send_sem.at[5], recv_sem.at[4], {"seq": me}).wait_recv()
        gate_sum = jnp.sum(gg[...], axis=0)[0:1]
        gg_home = dot_nt(jnp.where(of_home, gate_sum, 0.0).astype(BF16), lanes).astype(BF16)
        remote(gchk.at[pl.ds(0, WPH - 1)], gchk.at[pl.ds(0, WPH - 1)], send_sem.at[4], recv_sem.at[3], {"seq": me}).wait_recv()
        right_rows = dot(put_g, gg_home) + dot(put_o, gchk[...].reshape(CLS, HD))
        for n in range(1, WPH):
            other = lax.rem(cls + n, WPH)
            remote(psum.at[other], psum.at[other], send_sem.at[6], ps_sem.at[other], {"seq": me}).wait_recv()
            mine = mine + psum[other].astype(F32)
        mine = mine.astype(BF16)
        qv_rows = dot(put_q, jnp.concatenate([dqc, mine[:, HD:]], axis=1))
        k_rows = dot(put_k, mine[:, :HD])
        full = jnp.concatenate([qv_rows[:, :HD] + k_rows, qv_rows[:, HD:] + right_rows], axis=1)
        back[...] = full.astype(BF16).reshape(SEQ, MSG, 2 * HD)

        def send_back(n, carry):
            to = lax.rem(me + n, SEQ)
            remote(back.at[to], home.at[slot], send_sem.at[7], recv_sem.at[5], {"seq": to}).start()
            return carry

        lax.fori_loop(1, SEQ, send_back, 0)
        own_back = pltpu.make_async_copy(back.at[me], home.at[slot], loc_sem.at[1])
        own_back.start()

        remote(rows.at[pl.ds(0, workers - 1)], rows.at[pl.ds(0, workers - 1)], send_sem.at[1], recv_sem.at[1], {"seq": me}).wait_send()
        remote(kv.at[pl.ds(0, WPH - 1)], kv.at[pl.ds(0, WPH - 1)], send_sem.at[2], kv_sem.at[0], {"seq": me}).wait_send()
        remote(dsend.at[pl.ds(0, WPH - 1)], dcls.at[pl.ds(0, WPH - 1)], send_sem.at[3], recv_sem.at[2], {"seq": me}).wait_send()
        remote(gsend.at[pl.ds(0, WPH - 1)], gchk.at[pl.ds(0, WPH - 1)], send_sem.at[4], recv_sem.at[3], {"seq": me}).wait_send()
        if n_tp > 1:
            remote(others, others, send_sem.at[5], recv_sem.at[4], {"seq": me}).wait_send()
        remote(part.at[pl.ds(0, WPH - 1)], part.at[pl.ds(0, WPH - 1)], send_sem.at[6], ps_sem.at[0], {"seq": me}).wait_send()
        remote(back.at[pl.ds(0, SEQ - 1)], back.at[pl.ds(0, SEQ - 1)], send_sem.at[7], recv_sem.at[5], {"seq": me}).wait_send()
        own_back.wait()
        remote(home.at[pl.ds(0, workers - 1)], home.at[pl.ds(0, workers - 1)], send_sem.at[7], recv_sem.at[5], {"seq": me}).wait_recv()

    @pl.when(jnp.logical_not(is_worker))
    def _():
        remote(msg, msg, send_sem.at[1], recv_sem.at[1], {"seq": me}).wait_send()
        remote(home, home, send_sem.at[7], recv_sem.at[5], {"seq": me}).wait_recv()

    j = iota((256, 128), 0)
    col = iota((256, 128), 1)
    slot_j = j & 63
    from_cls = MSG * ((start + slot_j) & 7)
    at = jnp.where(j < 64, from_cls + (slot_j >> 3), from_cls + 8 + (slot_j >> 3))
    at = jnp.where(j < 128, at, from_cls + 12)
    at = jnp.where(j < 192, at, jnp.where(j < 224, MSG * (slot_j >> 2) + 8 + (slot_j & 3), -1))
    take = onehot(col == at)
    gate_rows = jnp.zeros((CAP, HD), F32)
    for k in range(heads):
        cols = slice(k * HD, (k + 1) * HD)
        res = dot(take, home[pl.ds(k * WPH, WPH)].reshape(WPH * MSG, 2 * HD))
        dq_ref[:, cols] = res[0:64, :HD].astype(BF16)
        dk_ref[:, cols] = res[64:128, :HD].astype(BF16)
        dv_ref[:, cols] = res[0:64, HD:].astype(BF16)
        gated_ref[:, cols] = res[192:224, HD:].astype(BF16)
        gate_rows = gate_rows + res[128:192, HD:]
    mine_lane = iota((CAP, HD), 1) == (iota((CAP, HD), 0) >> 3)
    gate_grad = jnp.sum(jnp.where(mine_lane, gate_rows, 0.0), axis=1, keepdims=True)
    logit_grad = gate_grad * gate_col * (1.0 - gate_col)
    router_ref[...] = jnp.sum(jnp.where(spots, jnp.broadcast_to(logit_grad, (CAP, TOK)), 0.0), axis=0, keepdims=True)
    remote(cnt.at[pl.ds(0, SEQ - 1)], cnt.at[pl.ds(0, SEQ - 1)], send_sem.at[0], recv_sem.at[0], {"seq": me}).wait_send()


def body(picked, owner_perm, router_logit, queries, keys, values, out_grad):
    n_tp = lax.axis_size("tp")
    heads = queries.shape[1] // HD
    width = heads * HD
    workers = heads * WPH
    vmem = pl.BlockSpec(memory_space=pltpu.VMEM)
    dma = pltpu.SemaphoreType.DMA
    gated, dq, dk, dv, router = pl.pallas_call(
        functools.partial(kernel, n_tp, heads),
        out_shape=(
            jax.ShapeDtypeStruct((out_grad.shape[0], width), BF16),
            jax.ShapeDtypeStruct((CAP, width), BF16),
            jax.ShapeDtypeStruct((CAP, width), BF16),
            jax.ShapeDtypeStruct((CAP, width), BF16),
            jax.ShapeDtypeStruct((1, TOK), F32),
        ),
        in_specs=[vmem] * 7,
        out_specs=[vmem] * 5,
        scratch_shapes=[
            pltpu.VMEM((1, 128), I32),
            pltpu.VMEM((SEQ, 1, 128), I32),
            pltpu.VMEM((workers, MSG, 2 * HD), BF16),
            pltpu.VMEM((SEQ, MSG, 2 * HD), BF16),
            pltpu.VMEM((1, CLS, HD), BF16),
            pltpu.VMEM((WPH, CLS, 2 * HD), BF16),
            pltpu.VMEM((WPH, 32, HD), BF16),
            pltpu.VMEM((WPH, 32, HD), BF16),
            pltpu.VMEM((WPH, CLS, CLS), F32),
            pltpu.VMEM((WPH, CLS, CLS), BF16),
            pltpu.VMEM((WPH, CLS, 2 * HD), BF16),
            pltpu.VMEM((WPH, CLS, 2 * HD), BF16),
            pltpu.VMEM((WPH, 32, HD), BF16),
            pltpu.VMEM((WPH, 32, HD), BF16),
            pltpu.VMEM((n_tp, 8, CLS), F32),
            pltpu.VMEM((SEQ, MSG, 2 * HD), BF16),
            pltpu.VMEM((workers, MSG, 2 * HD), BF16),
            dma((8,)),
            dma((6,)),
            dma((WPH,)),
            dma((WPH,)),
            dma((2,)),
        ],
        compiler_params=pltpu.CompilerParams(
            collective_id=0, has_side_effects=True, vmem_limit_bytes=48 * 1024 * 1024
        ),
    )(
        picked.reshape(1, CAP),
        owner_perm.reshape(1, SEQ),
        router_logit.reshape(1, TOK),
        queries,
        keys,
        values,
        out_grad,
    )
    return gated, dq, dk, dv, router.reshape(TOK)


def solution(mesh):
    return jax.shard_map(
        body,
        mesh=mesh,
        in_specs=(P("seq"), P(), P("seq"), P("seq", "tp"), P("seq", "tp"), P("seq", "tp"), P("seq", "tp")),
        out_specs=(P("seq", "tp"), P("seq", "tp"), P("seq", "tp"), P("seq", "tp"), P("seq")),
        check_vma=False,
    )
```

```python
import functools

import jax
import jax.numpy as jnp
from jax import lax
from jax.experimental import pallas as pl
from jax.experimental.pallas import tpu as pltpu
from jax.sharding import PartitionSpec as P

HD = 128
SEQ = 64
CAP = 64
TOK = 256
WPH = 8
CLS = 256
MSG = 16
SCALE = HD ** -0.5
MESH = pl.DeviceIdType.MESH
BF16, F32, I32 = jnp.bfloat16, jnp.float32, jnp.int32


def iota(shape, axis):
    return lax.broadcasted_iota(I32, shape, axis)


def onehot(hit):
    return jnp.where(hit, 1.0, 0.0).astype(BF16)


def dot(a, b):
    return lax.dot_general(a, b, (((1,), (0,)), ((), ())), preferred_element_type=F32)


def dot_nt(a, b):
    return lax.dot_general(a, b, (((1,), (1,)), ((), ())), preferred_element_type=F32)


def dot_tn(a, b):
    return lax.dot_general(a, b, (((0,), (0,)), ((), ())), preferred_element_type=F32)


def place_of(head, cls):
    z = head + head // 3
    return (cls // 2) * 16 + z * 2 + lax.rem(cls, 2)


def remote(src, dst, send, recv, device):
    return pltpu.make_async_remote_copy(
        src_ref=src, dst_ref=dst, send_sem=send, recv_sem=recv, device_id=device, device_id_type=MESH
    )


def find_logits(me, picked, logits):
    eye = iota((CAP, CAP), 0) == iota((CAP, CAP), 1)
    picked_col = jnp.sum(jnp.where(eye, jnp.broadcast_to(picked, (CAP, CAP)), 0), axis=1, keepdims=True)
    spots = jnp.broadcast_to(picked_col - me * TOK, (CAP, TOK)) == iota((CAP, TOK), 1)
    halves = logits.astype(F32)
    wide = jnp.broadcast_to(jnp.concatenate([halves[0:1], halves[1:2]], axis=1), (CAP, TOK))
    return spots, jnp.sum(jnp.where(spots, wide, 0.0), axis=1, keepdims=True)


def kernel(
    n_tp,
    heads,
    picked_in,
    perm_in,
    logit_in,
    q_in,
    k_in,
    v_in,
    d_in,
    start_ref,
    home_a,
    home_b,
    picked_ref,
    perm_ref,
    logit_ref,
    q_ref,
    k_ref,
    v_ref,
    d_ref,
    cnt_out,
    cnt,
    msg_a,
    msg_b,
    rows_a,
    rows_b,
    k_all,
    v_all,
    dsend,
    dcls,
    put,
    sbuf,
    pbuf,
    part_k,
    part_v,
    pre_k,
    pre_v,
    sum_k,
    sum_v,
    gsend,
    gchk,
    gg,
    back_a,
    back_b,
    in_sem,
    send_sem,
    recv_sem,
    k_sem,
    v_sem,
    pre_k_sem,
    pre_v_sem,
    sum_k_sem,
    sum_v_sem,
    loc_sem,
):
    me = lax.axis_index("seq")
    tp = lax.axis_index("tp")
    z = lax.rem(lax.div(me, 2), 8)
    core = lax.rem(me, 2)
    x = lax.div(me, 16)
    is_worker = lax.rem(z, 4) < 3
    head = z - lax.div(z, 4)
    cls = x * 2 + core
    slot = head * WPH + cls
    workers = heads * WPH
    sibling = {"seq": me + 1 - 2 * core}

    loads = [
        pltpu.make_async_copy(src, dst, in_sem.at[n])
        for n, (src, dst) in enumerate(
            zip(
                (picked_in, perm_in, logit_in, k_in, v_in, q_in, d_in),
                (picked_ref, perm_ref, logit_ref, k_ref, v_ref, q_ref, d_ref),
            )
        )
    ]
    for load in loads:
        load.start()

    barrier = pltpu.get_barrier_semaphore()

    def greet(n, carry):
        pl.semaphore_signal(barrier, inc=1, device_id={"seq": lax.rem(me + n, SEQ)}, device_id_type=MESH)
        return carry

    lax.fori_loop(1, SEQ, greet, 0)
    for n in range(1, n_tp):
        pl.semaphore_signal(barrier, inc=1, device_id={"tp": lax.rem(tp + n, n_tp)}, device_id_type=MESH)

    loads[0].wait()
    picked = picked_ref[...]
    count = jnp.sum(jnp.where(picked >= 0, 1, 0), axis=1, keepdims=True)
    cnt_out[...] = jnp.broadcast_to(count, (1, 128))
    pl.semaphore_wait(barrier, SEQ - 1 + n_tp - 1)

    def send_count(n, carry):
        remote(cnt_out, cnt.at[me], send_sem.at[0], recv_sem.at[0], {"seq": lax.rem(me + n, SEQ)}).start()
        return carry

    lax.fori_loop(1, SEQ, send_count, 0)
    cnt[me] = cnt_out[...]

    for load in loads[1:]:
        load.wait()
    spots, logit_col = find_logits(me, picked, logit_ref[...])
    spread = jnp.where(iota((CAP, 128), 1) == (iota((CAP, 128), 0) >> 3), jnp.broadcast_to(logit_col, (CAP, 128)), 0.0)
    spread = spread.astype(BF16)
    fill = jnp.zeros((32, HD), BF16)

    counted = cnt.at[pl.ds(0, SEQ - 1)]
    remote(counted, counted, send_sem.at[0], recv_sem.at[0], sibling).wait_recv()
    counts = jnp.sum(cnt[...], axis=1)
    start = jnp.sum(jnp.where(iota((SEQ, 128), 0) < me, counts, 0), axis=0, keepdims=True)
    start_ref[...] = start

    n_out = iota((WPH * MSG, 128), 0)
    t_out = n_out & 15
    turn = ((n_out >> 4) - start) & 7
    src = iota((WPH * MSG, 128), 1)
    pick_a = onehot(src == 8 * t_out + turn)
    b_from = jnp.where(t_out < 8, 8 * t_out + turn, jnp.where(t_out < 12, CAP + 4 * (n_out >> 4) + t_out - 8, -1))
    pick_b = onehot(src == b_from)
    src64 = iota((WPH * MSG, CAP), 1)
    pick_logit = onehot((t_out[:, :CAP] == 12) & ((src64 & 7) == turn[:, :CAP]))

    def send_rows(msg, rows, sem):
        def send_one(n, carry):
            w = lax.rem(n + me, workers)
            dst = place_of(lax.div(w, WPH), lax.rem(w, WPH))

            @pl.when(dst != me)
            def _():
                remote(msg.at[w], rows.at[me], send_sem.at[sem], recv_sem.at[sem], {"seq": dst}).start()

            return carry

        lax.fori_loop(0, workers, send_one, 0)

    for k in range(heads):
        cols = slice(k * HD, (k + 1) * HD)
        both = dot(pick_a, jnp.concatenate([k_ref[:, cols], q_ref[:, cols]], axis=0))
        msg_a[pl.ds(k * WPH, WPH)] = both.astype(BF16).reshape(WPH, MSG, HD)
    send_rows(msg_a, rows_a, 1)
    logit_rows = dot(pick_logit, spread)
    for k in range(heads):
        cols = slice(k * HD, (k + 1) * HD)
        both = dot(pick_b, jnp.concatenate([v_ref[:, cols], d_ref[:, cols], fill], axis=0)) + logit_rows
        msg_b[pl.ds(k * WPH, WPH)] = both.astype(BF16).reshape(WPH, MSG, HD)
    send_rows(msg_b, rows_b, 2)

    @pl.when(is_worker)
    def _():
        left = []

        def gone(src, sem):
            left.append((src, sem))

        def done():
            for src, sem in left:
                remote(src, src, send_sem.at[sem], recv_sem.at[0], sibling).wait_send()

        def came(ref, sem):
            remote(ref, ref, send_sem.at[0], sem, sibling).wait_recv()

        own_a = pltpu.make_async_copy(msg_a.at[slot], rows_a.at[me], loc_sem.at[0])
        own_a.start()
        own_b = pltpu.make_async_copy(msg_b.at[slot], rows_b.at[me], loc_sem.at[1])
        own_b.start()
        gone(msg_a.at[pl.ds(0, workers - 1)], 1)
        gone(msg_b.at[pl.ds(0, workers - 1)], 2)

        def peer(n, flip):
            return lax.rem(x + n, 4) * 2 + (1 - core if flip else core)

        def send_all(ref, sems, sem):
            remote(ref.at[cls], ref.at[cls], send_sem.at[sem], sems.at[cls], sibling).start()
            for n in (1, 3, 2):
                dst = {"seq": place_of(head, peer(n, 0))}
                remote(ref.at[cls], ref.at[cls], send_sem.at[sem], sems.at[cls], dst).start()
            gone(ref.at[pl.ds(0, 4)], sem)

        def pass_on(ref, sems, sem, n):
            block = ref.at[peer(n, 0)]
            came(block, sems.at[peer(n, 0)])
            remote(block, block, send_sem.at[sem], sems.at[peer(n, 0)], sibling).start()

        n_row = iota((SEQ, SEQ * MSG), 1)
        below = jnp.concatenate([counts] * 8, axis=1)
        at_h = iota((SEQ, SEQ * MSG), 0)
        start_n = jnp.sum(jnp.where(at_h < (n_row >> 4), below, 0), axis=0, keepdims=True)
        end_n = jnp.sum(jnp.where(at_h <= (n_row >> 4), below, 0), axis=0, keepdims=True)
        t_n = iota((1, SEQ * MSG), 1) & 15
        p_n = ((start_n - cls + 7) >> 3) + (t_n & 7)
        live_n = p_n < ((end_n - cls + 7) >> 3)
        lo_at = jnp.where(live_n & (t_n < 8), p_n, -1)
        hi_at = jnp.where(live_n & (t_n >= 8), p_n, -1)
        p_sub = iota((CLS, SEQ * MSG), 0)
        take_lo = onehot(p_sub == lo_at)
        take_hi = onehot(p_sub == hi_at)

        came(rows_a.at[pl.ds(0, SEQ - 1)], recv_sem.at[1])
        own_a.wait()
        a_rows = rows_a[...].reshape(SEQ * MSG, HD)
        k_all[cls] = dot(take_lo, a_rows).astype(BF16)
        send_all(k_all, k_sem, 3)
        q = dot(take_hi, a_rows).astype(BF16)

        m_sub = iota((CLS, SEQ), 0)
        residue_m = 8 * (m_sub & 7) + (m_sub >> 5)
        perm = jnp.broadcast_to(perm_ref[...], (CLS, SEQ))
        owner_m = jnp.sum(jnp.where(iota((CLS, SEQ), 1) == residue_m, perm, 0), axis=1, keepdims=True)
        d_at = MSG * owner_m + 8 + ((iota((CLS, 1), 0) & 31) >> 3)
        take_d = onehot(iota((CLS, SEQ * MSG), 1) == d_at)
        take_l = onehot(n_row == MSG * at_h + 12)
        tri = onehot(iota((SEQ, SEQ), 1) < iota((SEQ, SEQ), 0))
        starts = dot(tri, counts.astype(BF16)).astype(I32)
        base = (starts - cls + 7) >> 3
        after = (starts + counts - cls + 7) >> 3
        base2 = jnp.concatenate([base, base], axis=1)
        after2 = jnp.concatenate([after, after], axis=1)
        p_lane = iota((SEQ, CLS), 1)
        of_home = (base2 <= p_lane) & (p_lane < after2)
        lane_p = jnp.sum(jnp.where(of_home, p_lane - base2, 0), axis=0, keepdims=True)
        lanes = onehot(iota((128, CLS), 0) == lane_p)

        n_sub = iota((SEQ * MSG, SEQ), 0)
        rep = onehot((n_sub >> 4) == iota((SEQ * MSG, SEQ), 1))
        perm_o = jnp.broadcast_to(perm_ref[...], (SEQ, SEQ))
        res_o = jnp.sum(jnp.where(perm_o == iota((SEQ, SEQ), 0), iota((SEQ, SEQ), 1), 0), axis=1, keepdims=True)
        three = jnp.concatenate([base, after, jnp.broadcast_to(res_o, (SEQ, 128))], axis=1).astype(F32).astype(BF16)
        wide = dot(rep, three).astype(I32)
        t_col = iota((SEQ * MSG, 128), 0) & 15
        p_col = wide[:, :128] + (t_col & 7)
        live_col = p_col < wide[:, 128:256]
        res_col = wide[:, 256:]
        lo_to = jnp.where(live_col & (t_col < 8), p_col, -1)
        hi_to = jnp.where(live_col & (t_col >= 8), p_col, -1)
        o_to = jnp.where((t_col >= 8) & (t_col < 12), 32 * (res_col & 7) + 8 * (t_col - 8) + (res_col >> 3), -1)
        p_at = iota((SEQ * MSG, CLS), 1)
        put[0] = onehot(p_at == jnp.concatenate([lo_to, lo_to], axis=1))
        put[1] = onehot(p_at == jnp.concatenate([hi_to, hi_to], axis=1))
        put[2] = onehot(p_at == jnp.concatenate([o_to, o_to], axis=1))
        put_g = onehot(iota((SEQ * MSG, SEQ), 0) == MSG * iota((SEQ * MSG, SEQ), 1) + 12)

        came(rows_b.at[pl.ds(0, SEQ - 1)], recv_sem.at[2])
        own_b.wait()
        b_rows = rows_b[...].reshape(SEQ * MSG, HD)
        v_all[cls] = dot(take_lo, b_rows).astype(BF16)
        send_all(v_all, v_sem, 4)
        dsend[...] = dot(take_d, b_rows).astype(BF16).reshape(WPH, 32, HD)

        def send_d(n, carry):
            to = lax.rem(cls + n, WPH)
            remote(dsend.at[to], dcls.at[cls], send_sem.at[6], recv_sem.at[3], {"seq": place_of(head, to)}).start()
            return carry

        lax.fori_loop(1, WPH, send_d, 0)
        dcls[cls] = dsend[cls]
        gone(dsend.at[pl.ds(0, WPH - 1)], 6)
        for n in (1, 3):
            pass_on(k_all, k_sem, 5, n)
        logit_h = dot(take_l, b_rows).astype(BF16)
        logit_p = jnp.sum(jnp.where(of_home, dot(logit_h, lanes), 0.0), axis=0, keepdims=True)
        gate = 1.0 / (1.0 + jnp.exp(-logit_p))

        top = jnp.full((1, CLS), -jnp.inf, F32)
        k_sub, q_lane = iota((CLS, CLS), 0), iota((CLS, CLS), 1)
        order = ((0, 0), (0, 1), (1, 0), (3, 0), (1, 1), (3, 1), (2, 0), (2, 1))
        for n, flip in order:
            other = peer(n, flip)
            if (n, flip) == (1, 0):
                pass_on(k_all, k_sem, 5, 2)
            if flip:
                came(k_all.at[other], k_sem.at[other])
            later = jnp.where(other > cls, 1, 0)
            s = dot_nt(k_all[other], q) * SCALE
            s = jnp.where(k_sub + later <= q_lane, s, -1e30)
            sbuf[2 * n + flip] = s
            top = jnp.maximum(top, jnp.max(s, axis=0, keepdims=True))
        gone(k_all.at[pl.ds(0, 3)], 5)
        total = jnp.zeros((1, CLS), F32)
        for n in range(WPH):
            e = jnp.exp(sbuf[n] - top)
            sbuf[n] = e
            total = total + jnp.sum(e, axis=0, keepdims=True)
        inv = 1.0 / total
        for n in range(WPH):
            w = sbuf[n] * inv
            sbuf[n] = w
            pbuf[n] = w.astype(BF16)

        came(dcls.at[pl.ds(0, WPH - 1)], recv_sem.at[3])
        dy_t = dcls[...].reshape(CLS, HD).astype(F32).T
        dor_t = (dy_t * gate).astype(BF16).astype(F32)
        dor = dor_t.T.astype(BF16)

        def to_sibling(grads, part, pre, sems, sem, n):
            part[2 * n + 1] = grads.astype(BF16)
            remote(part.at[2 * n + 1], pre.at[n], send_sem.at[sem], sems.at[n], sibling).start()

        def to_class(grads, part, pre, pre_sems, total, sems, sem, n):
            came(pre.at[n], pre_sems.at[n])
            grads = grads + pre[n].astype(F32)
            if n:
                part[2 * n] = grads.astype(BF16)
                dst = {"seq": place_of(head, peer(n, 0))}
                remote(part.at[2 * n], total.at[x], send_sem.at[sem], sems.at[x], dst).start()
            return grads

        def collect(mine, total, sems):
            for n in (1, 3, 2):
                there = lax.rem(x + n, 4)
                came(total.at[there], sems.at[there])
                mine = mine + total[there].astype(F32)
            return mine.astype(BF16)

        far_first = (2, 1, 3, 0)
        for n in far_first:
            to_sibling(dot(pbuf[2 * n + 1], dor), part_v, pre_v, pre_v_sem, 9, n)
        gone(part_v.at[pl.ds(0, 4)], 9)
        for n in (1, 3):
            pass_on(v_all, v_sem, 7, n)
        for n in far_first:
            mine_v = to_class(dot(pbuf[2 * n], dor), part_v, pre_v, pre_v_sem, sum_v, sum_v_sem, 10, n)
        gone(part_v.at[pl.ds(0, 3)], 10)
        pass_on(v_all, v_sem, 7, 2)
        gone(v_all.at[pl.ds(0, 3)], 7)
        out_t = jnp.zeros((HD, CLS), F32)
        for n, flip in order:
            other = peer(n, flip)
            if flip:
                came(v_all.at[other], v_sem.at[other])
            out_t = out_t + dot_tn(v_all[other], pbuf[2 * n + flip])
        delta = jnp.sum(dor_t * out_t, axis=0, keepdims=True)
        gate_grad = jnp.sum(dy_t * out_t, axis=0, keepdims=True)
        gsend[...] = (out_t * gate).T.astype(BF16).reshape(WPH, 32, HD)
        gg[tp] = jnp.broadcast_to(gate_grad, (8, CLS))

        def send_gated(n, carry):
            to = lax.rem(cls + n, WPH)
            remote(gsend.at[to], gchk.at[cls], send_sem.at[8], recv_sem.at[4], {"seq": place_of(head, to)}).start()
            return carry

        lax.fori_loop(1, WPH, send_gated, 0)
        gchk[cls] = gsend[cls]
        gone(gsend.at[pl.ds(0, WPH - 1)], 8)
        if n_tp > 1:
            for n in range(1, n_tp):
                remote(gg.at[tp], gg.at[tp], send_sem.at[13], recv_sem.at[5], {"tp": lax.rem(tp + n, n_tp)}).start()
            gone(gg.at[pl.ds(0, n_tp - 1)], 13)

        dq_t = jnp.zeros((HD, CLS), F32)
        for flip in (1, 0):
            for n in far_first:
                other = peer(n, flip)
                dp = dot_nt(v_all[other], dor)
                ds = (sbuf[2 * n + flip] * (dp - delta)).astype(BF16)
                dq_t = dq_t + dot_tn(k_all[other], ds)
                grads = dot(ds, q) * SCALE
                if flip:
                    to_sibling(grads, part_k, pre_k, pre_k_sem, 11, n)
                else:
                    mine_k = to_class(grads, part_k, pre_k, pre_k_sem, sum_k, sum_k_sem, 12, n)
        gone(part_k.at[pl.ds(0, 4)], 11)
        gone(part_k.at[pl.ds(0, 3)], 12)

        def send_back(back, home, sem):
            def send_one(n, carry):
                to = lax.rem(me + n, SEQ)
                remote(back.at[to], home.at[slot], send_sem.at[sem], recv_sem.at[sem - 8], {"seq": to}).start()
                return carry

            lax.fori_loop(1, SEQ, send_one, 0)
            gone(back.at[pl.ds(0, SEQ - 1)], sem)

        dqc = (dq_t * SCALE).T.astype(BF16)
        mine_v = collect(mine_v, sum_v, sum_v_sem)
        full = dot(put[0], mine_v) + dot(put[1], dqc)
        back_a[...] = full.astype(BF16).reshape(SEQ, MSG, HD)
        send_back(back_a, home_a, 14)
        own_a = pltpu.make_async_copy(back_a.at[me], home_a.at[slot], loc_sem.at[0])
        own_a.start()
        if n_tp > 1:
            came(gg.at[pl.ds(0, n_tp - 1)], recv_sem.at[5])
        gate_sum = jnp.sum(gg[...], axis=0)[0:1]
        gg_home = dot_nt(jnp.where(of_home, gate_sum, 0.0).astype(BF16), lanes).astype(BF16)
        came(gchk.at[pl.ds(0, WPH - 1)], recv_sem.at[4])
        rest = dot(put_g, gg_home) + dot(put[2], gchk[...].reshape(CLS, HD))
        mine_k = collect(mine_k, sum_k, sum_k_sem)
        full = dot(put[0], mine_k) + rest
        back_b[...] = full.astype(BF16).reshape(SEQ, MSG, HD)
        send_back(back_b, home_b, 15)
        own_b = pltpu.make_async_copy(back_b.at[me], home_b.at[slot], loc_sem.at[1])
        own_b.start()
        done()
        own_a.wait()
        own_b.wait()
        came(home_a.at[pl.ds(0, workers - 1)], recv_sem.at[6])
        came(home_b.at[pl.ds(0, workers - 1)], recv_sem.at[7])

    @pl.when(jnp.logical_not(is_worker))
    def _():
        remote(msg_a, msg_a, send_sem.at[1], recv_sem.at[1], sibling).wait_send()
        remote(msg_b, msg_b, send_sem.at[2], recv_sem.at[2], sibling).wait_send()
        remote(home_a, home_a, send_sem.at[14], recv_sem.at[6], sibling).wait_recv()
        remote(home_b, home_b, send_sem.at[15], recv_sem.at[7], sibling).wait_recv()

    remote(counted, counted, send_sem.at[0], recv_sem.at[0], sibling).wait_send()


def finish(
    heads, picked_ref, logit_ref, start_ref, home_a, home_b, gated_ref, dq_ref, dk_ref, dv_ref, router_ref
):
    me = lax.axis_index("seq")
    start = start_ref[...]
    spots, logit_col = find_logits(me, picked_ref[...], logit_ref[...])
    gate_col = 1.0 / (1.0 + jnp.exp(-logit_col))
    col = iota((CAP, 128), 1)
    j = iota((CAP, 128), 0)
    from_cls = MSG * ((start + j) & 7)
    lo = from_cls + (j >> 3)
    take_lo = col == lo
    take_hi = col == lo + 8
    take_g = col == from_cls + 12
    take_o = (col == MSG * (j >> 2) + 8 + (j & 3)) & (j < 32)
    take_a = jnp.concatenate([onehot(take_lo), onehot(take_hi)], axis=0)
    take_b = jnp.concatenate([onehot(take_lo), onehot(take_g), onehot(take_o)], axis=0)
    gate_rows = jnp.zeros((CAP, HD), F32)
    for k in range(heads):
        cols = slice(k * HD, (k + 1) * HD)
        res = dot(take_a, home_a[pl.ds(k * WPH, WPH)].reshape(WPH * MSG, HD))
        dv_ref[:, cols] = res[0:64].astype(BF16)
        dq_ref[:, cols] = res[64:128].astype(BF16)
        res = dot(take_b, home_b[pl.ds(k * WPH, WPH)].reshape(WPH * MSG, HD))
        dk_ref[:, cols] = res[0:64].astype(BF16)
        gated_ref[:, cols] = res[128:160].astype(BF16)
        gate_rows = gate_rows + res[64:128]
    mine_lane = iota((CAP, HD), 1) == (iota((CAP, HD), 0) >> 3)
    gate_grad = jnp.sum(jnp.where(mine_lane, gate_rows, 0.0), axis=1, keepdims=True)
    logit_grad = gate_grad * gate_col * (1.0 - gate_col)
    router_ref[...] = jnp.sum(jnp.where(spots, jnp.broadcast_to(logit_grad, (CAP, TOK)), 0.0), axis=0, keepdims=True)


def body(picked, owner_perm, router_logit, queries, keys, values, out_grad):
    n_tp = lax.axis_size("tp")
    heads = queries.shape[1] // HD
    width = heads * HD
    workers = heads * WPH
    picks = out_grad.shape[0]
    vmem = pl.BlockSpec(memory_space=pltpu.VMEM)
    hbm = pl.BlockSpec(memory_space=pltpu.HBM)
    dma = pltpu.SemaphoreType.DMA
    picked = picked.reshape(1, CAP)
    router_logit = router_logit.reshape(2, TOK // 2)
    start, home_a, home_b = pl.pallas_call(
        functools.partial(kernel, n_tp, heads),
        out_shape=(
            jax.ShapeDtypeStruct((1, 128), I32),
            jax.ShapeDtypeStruct((workers, MSG, HD), BF16),
            jax.ShapeDtypeStruct((workers, MSG, HD), BF16),
        ),
        in_specs=[hbm] * 7,
        out_specs=[vmem, hbm, hbm],
        scratch_shapes=[
            pltpu.VMEM((1, CAP), I32),
            pltpu.VMEM((1, SEQ), I32),
            pltpu.VMEM((2, TOK // 2), BF16),
            pltpu.VMEM((CAP, width), BF16),
            pltpu.VMEM((CAP, width), BF16),
            pltpu.VMEM((CAP, width), BF16),
            pltpu.VMEM((picks, width), BF16),
            pltpu.VMEM((1, 128), I32),
            pltpu.VMEM((SEQ, 1, 128), I32),
            pltpu.VMEM((workers, MSG, HD), BF16),
            pltpu.VMEM((workers, MSG, HD), BF16),
            pltpu.VMEM((SEQ, MSG, HD), BF16),
            pltpu.VMEM((SEQ, MSG, HD), BF16),
            pltpu.VMEM((WPH, CLS, HD), BF16),
            pltpu.VMEM((WPH, CLS, HD), BF16),
            pltpu.VMEM((WPH, 32, HD), BF16),
            pltpu.VMEM((WPH, 32, HD), BF16),
            pltpu.VMEM((3, SEQ * MSG, CLS), BF16),
            pltpu.VMEM((WPH, CLS, CLS), F32),
            pltpu.VMEM((WPH, CLS, CLS), BF16),
            pltpu.VMEM((WPH, CLS, HD), BF16),
            pltpu.VMEM((WPH, CLS, HD), BF16),
            pltpu.VMEM((4, CLS, HD), BF16),
            pltpu.VMEM((4, CLS, HD), BF16),
            pltpu.VMEM((4, CLS, HD), BF16),
            pltpu.VMEM((4, CLS, HD), BF16),
            pltpu.VMEM((WPH, 32, HD), BF16),
            pltpu.VMEM((WPH, 32, HD), BF16),
            pltpu.VMEM((n_tp, 8, CLS), F32),
            pltpu.VMEM((SEQ, MSG, HD), BF16),
            pltpu.VMEM((SEQ, MSG, HD), BF16),
            dma((7,)),
            dma((16,)),
            dma((8,)),
            dma((WPH,)),
            dma((WPH,)),
            dma((4,)),
            dma((4,)),
            dma((4,)),
            dma((4,)),
            dma((2,)),
        ],
        compiler_params=pltpu.CompilerParams(
            collective_id=0, has_side_effects=True, vmem_limit_bytes=60 * 1024 * 1024
        ),
    )(
        picked,
        owner_perm.reshape(1, SEQ),
        router_logit,
        queries,
        keys,
        values,
        out_grad,
    )
    gated, dq, dk, dv, router = pl.pallas_call(
        functools.partial(finish, heads),
        out_shape=(
            jax.ShapeDtypeStruct((picks, width), BF16),
            jax.ShapeDtypeStruct((CAP, width), BF16),
            jax.ShapeDtypeStruct((CAP, width), BF16),
            jax.ShapeDtypeStruct((CAP, width), BF16),
            jax.ShapeDtypeStruct((1, TOK), F32),
        ),
        in_specs=[vmem] * 5,
        out_specs=[vmem] * 5,
        compiler_params=pltpu.CompilerParams(vmem_limit_bytes=60 * 1024 * 1024),
    )(picked, router_logit, start, home_a, home_b)
    return gated, dq, dk, dv, router.reshape(TOK)


def solution(mesh):
    return jax.shard_map(
        body,
        mesh=mesh,
        in_specs=(P("seq"), P(), P("seq"), P("seq", "tp"), P("seq", "tp"), P("seq", "tp"), P("seq", "tp")),
        out_specs=(P("seq", "tp"), P("seq", "tp"), P("seq", "tp"), P("seq", "tp"), P("seq")),
        check_vma=False,
    )
```

```python
import functools

import jax
import jax.numpy as jnp
from jax import lax
from jax.experimental import pallas as pl
from jax.experimental.pallas import tpu as pltpu
from jax.sharding import PartitionSpec as P

HD = 128
SEQ = 64
CAP = 64
TOK = 256
WPH = 8
CLS = 256
MSG = 16
SCALE = HD ** -0.5
SCALE_LOG2 = SCALE * 1.4426950408889634
MESH = pl.DeviceIdType.MESH
BF16, F32, I32 = jnp.bfloat16, jnp.float32, jnp.int32


def iota(shape, axis):
    return lax.broadcasted_iota(I32, shape, axis)


def onehot(hit):
    return jnp.where(hit, 1.0, 0.0).astype(BF16)


def dot(a, b):
    return lax.dot_general(a, b, (((1,), (0,)), ((), ())), preferred_element_type=F32)


def dot_nt(a, b):
    return lax.dot_general(a, b, (((1,), (1,)), ((), ())), preferred_element_type=F32)


def dot_tn(a, b):
    return lax.dot_general(a, b, (((0,), (0,)), ((), ())), preferred_element_type=F32)


def place_of(head, cls):
    z = head + head // 3
    return (cls // 2) * 16 + z * 2 + lax.rem(cls, 2)


def remote(src, dst, send, recv, device):
    return pltpu.make_async_remote_copy(
        src_ref=src, dst_ref=dst, send_sem=send, recv_sem=recv, device_id=device, device_id_type=MESH
    )


def find_logits(me, picked, logits):
    eye = iota((CAP, CAP), 0) == iota((CAP, CAP), 1)
    picked_col = jnp.sum(jnp.where(eye, jnp.broadcast_to(picked, (CAP, CAP)), 0), axis=1, keepdims=True)
    spots = jnp.broadcast_to(picked_col - me * TOK, (CAP, TOK)) == iota((CAP, TOK), 1)
    halves = logits.astype(F32)
    wide = jnp.broadcast_to(jnp.concatenate([halves[0:1], halves[1:2]], axis=1), (CAP, TOK))
    return spots, jnp.sum(jnp.where(spots, wide, 0.0), axis=1, keepdims=True)


def kernel(
    n_tp,
    heads,
    picked_in,
    perm_in,
    logit_in,
    q_in,
    k_in,
    v_in,
    d_in,
    start_ref,
    gate_ref,
    home_c_out,
    home_q,
    home_b,
    picked_ref,
    perm_ref,
    logit_ref,
    q_ref,
    k_ref,
    v_ref,
    d_ref,
    cnt_out,
    cnt,
    msg_k,
    msg_v,
    msg_b,
    rows_k,
    rows_v,
    rows_b,
    k_all,
    v_all,
    dsend,
    dcls,
    put,
    put_e,
    sbuf,
    pbuf,
    part_k,
    part_v,
    pre_k,
    pre_v,
    sum_k,
    sum_v,
    gsend,
    gchk,
    gg,
    back_q,
    back_c,
    back_b,
    home_c,
    in_sem,
    send_sem,
    recv_sem,
    k_sem,
    v_sem,
    pre_k_sem,
    pre_v_sem,
    sum_k_sem,
    sum_v_sem,
    loc_sem,
):
    me = lax.axis_index("seq")
    tp = lax.axis_index("tp")
    z = lax.rem(lax.div(me, 2), 8)
    core = lax.rem(me, 2)
    x = lax.div(me, 16)
    is_worker = lax.rem(z, 4) < 3
    head = z - lax.div(z, 4)
    cls = x * 2 + core
    slot = head * WPH + cls
    workers = heads * WPH
    sibling = {"seq": me + 1 - 2 * core}

    loads = [
        pltpu.make_async_copy(src, dst, in_sem.at[n])
        for n, (src, dst) in enumerate(
            zip(
                (picked_in, perm_in, logit_in, k_in, v_in, q_in, d_in),
                (picked_ref, perm_ref, logit_ref, k_ref, v_ref, q_ref, d_ref),
            )
        )
    ]
    for load in loads:
        load.start()

    barrier = pltpu.get_barrier_semaphore()

    def greet(n, carry):
        pl.semaphore_signal(barrier, inc=1, device_id={"seq": lax.rem(me + n, SEQ)}, device_id_type=MESH)
        return carry

    lax.fori_loop(1, SEQ, greet, 0)
    for n in range(1, n_tp):
        pl.semaphore_signal(barrier, inc=1, device_id={"tp": lax.rem(tp + n, n_tp)}, device_id_type=MESH)

    loads[0].wait()
    picked = picked_ref[...]
    count = jnp.sum(jnp.where(picked >= 0, 1, 0), axis=1, keepdims=True)
    cnt_out[...] = jnp.broadcast_to(count, (1, 128))
    pl.semaphore_wait(barrier, SEQ - 1 + n_tp - 1)

    def send_count(n, carry):
        remote(cnt_out, cnt.at[me], send_sem.at[0], recv_sem.at[0], {"seq": lax.rem(me + n, SEQ)}).start()
        return carry

    lax.fori_loop(1, SEQ, send_count, 0)
    cnt[me] = cnt_out[...]

    for load in loads[1:]:
        load.wait()
    spots, logit_col = find_logits(me, picked, logit_ref[...])
    spread = jnp.where(iota((CAP, 128), 1) == (iota((CAP, 128), 0) >> 3), jnp.broadcast_to(logit_col, (CAP, 128)), 0.0)
    spread = spread.astype(BF16)
    fill = jnp.zeros((32, HD), BF16)

    counted = cnt.at[pl.ds(0, SEQ - 1)]
    remote(counted, counted, send_sem.at[0], recv_sem.at[0], sibling).wait_recv()
    counts = jnp.sum(cnt[...], axis=1)
    start = jnp.sum(jnp.where(iota((SEQ, 128), 0) < me, counts, 0), axis=0, keepdims=True)
    start_ref[...] = start

    n_half = iota((WPH * 8, CAP), 0)
    turn_half = ((n_half >> 3) - start[:, :CAP]) & 7
    pick_half = onehot(iota((WPH * 8, CAP), 1) == 8 * (n_half & 7) + turn_half)
    n_out = iota((WPH * MSG, 128), 0)
    t_out = n_out & 15
    turn = ((n_out >> 4) - start) & 7
    src = iota((WPH * MSG, 128), 1)
    b_from = jnp.where(t_out < 8, 8 * t_out + turn, jnp.where(t_out < 12, CAP + 4 * (n_out >> 4) + t_out - 8, -1))
    pick_b = onehot(src == b_from)
    src64 = iota((WPH * MSG, CAP), 1)
    pick_logit = onehot((t_out[:, :CAP] == 12) & ((src64 & 7) == turn[:, :CAP]))

    def send_rows(msg, rows, sem, recv):
        def send_one(n, carry):
            w = lax.rem(n + me, workers)
            dst = place_of(lax.div(w, WPH), lax.rem(w, WPH))

            @pl.when(dst != me)
            def _():
                remote(msg.at[w], rows.at[me], send_sem.at[sem], recv_sem.at[recv], {"seq": dst}).start()

            return carry

        lax.fori_loop(0, workers, send_one, 0)

    for ref, msg, rows, sem, recv in ((k_ref, msg_k, rows_k, 1, 1), (v_ref, msg_v, rows_v, 16, 8)):
        turned = dot(pick_half, ref[...]).astype(BF16)
        for k in range(heads):
            msg[pl.ds(k * WPH, WPH)] = turned[:, k * HD : (k + 1) * HD].reshape(WPH, 8, HD)
        send_rows(msg, rows, sem, recv)
    logit_rows = dot(pick_logit, spread)
    for k in range(heads):
        cols = slice(k * HD, (k + 1) * HD)
        both = dot(pick_b, jnp.concatenate([q_ref[:, cols], d_ref[:, cols], fill], axis=0)) + logit_rows
        msg_b[pl.ds(k * WPH, WPH)] = both.astype(BF16).reshape(WPH, MSG, HD)
    send_rows(msg_b, rows_b, 2, 2)
    left = []

    def gone(src, sem):
        left.append((src, sem))

    def done():
        for src, sem in left:
            remote(src, src, send_sem.at[sem], recv_sem.at[0], sibling).wait_send()

    def came(ref, sem):
        remote(ref, ref, send_sem.at[0], sem, sibling).wait_recv()

    @pl.when(is_worker)
    def _():
        own_k = pltpu.make_async_copy(msg_k.at[slot], rows_k.at[me], loc_sem.at[0])
        own_k.start()
        own_v = pltpu.make_async_copy(msg_v.at[slot], rows_v.at[me], loc_sem.at[3])
        own_v.start()
        own_b = pltpu.make_async_copy(msg_b.at[slot], rows_b.at[me], loc_sem.at[1])
        own_b.start()
        gone(msg_k.at[pl.ds(0, workers - 1)], 1)
        gone(msg_v.at[pl.ds(0, workers - 1)], 16)
        gone(msg_b.at[pl.ds(0, workers - 1)], 2)

        def peer(n, flip):
            return lax.rem(x + n, 4) * 2 + (1 - core if flip else core)

        def send_all(ref, sems, sem):
            remote(ref.at[cls], ref.at[cls], send_sem.at[sem], sems.at[cls], sibling).start()
            for n in (1, 3, 2):
                dst = {"seq": place_of(head, peer(n, 0))}
                remote(ref.at[cls], ref.at[cls], send_sem.at[sem], sems.at[cls], dst).start()
            gone(ref.at[pl.ds(0, 4)], sem)

        def pass_on(ref, sems, sem, n):
            block = ref.at[peer(n, 0)]
            came(block, sems.at[peer(n, 0)])
            remote(block, block, send_sem.at[sem], sems.at[peer(n, 0)], sibling).start()

        n_row = iota((SEQ, SEQ * MSG), 1)
        below = jnp.concatenate([counts] * 8, axis=1)
        at_h = iota((SEQ, SEQ * MSG), 0)
        start_n = jnp.sum(jnp.where(at_h < (n_row >> 4), below, 0), axis=0, keepdims=True)
        end_n = jnp.sum(jnp.where(at_h <= (n_row >> 4), below, 0), axis=0, keepdims=True)
        t_n = iota((1, SEQ * MSG), 1) & 15
        p_n = ((start_n - cls + 7) >> 3) + (t_n & 7)
        live_n = p_n < ((end_n - cls + 7) >> 3)
        lo_at = jnp.where(live_n & (t_n < 8), p_n, -1)
        p_sub = iota((CLS, SEQ * MSG), 0)
        take_lo = onehot(p_sub == lo_at)

        n_eight = iota((SEQ, SEQ * 8), 1)
        start_e = jnp.sum(jnp.where(at_h[:, : SEQ * 8] < (n_eight >> 3), below[:, : SEQ * 8], 0), axis=0, keepdims=True)
        end_e = jnp.sum(jnp.where(at_h[:, : SEQ * 8] <= (n_eight >> 3), below[:, : SEQ * 8], 0), axis=0, keepdims=True)
        p_e = ((start_e - cls + 7) >> 3) + (n_eight[0:1] & 7)
        e_at = jnp.where(p_e < ((end_e - cls + 7) >> 3), p_e, -1)
        take_eight = onehot(p_sub[:, : SEQ * 8] == e_at)

        came(rows_k.at[pl.ds(0, SEQ - 1)], recv_sem.at[1])
        own_k.wait()
        k_all[cls] = dot(take_eight, rows_k[...].reshape(SEQ * 8, HD)).astype(BF16)
        send_all(k_all, k_sem, 3)
        came(rows_v.at[pl.ds(0, SEQ - 1)], recv_sem.at[8])
        own_v.wait()
        v_all[cls] = dot(take_eight, rows_v[...].reshape(SEQ * 8, HD)).astype(BF16)
        send_all(v_all, v_sem, 4)

        m_sub = iota((CLS, SEQ), 0)
        residue_m = 8 * (m_sub & 7) + (m_sub >> 5)
        perm = jnp.broadcast_to(perm_ref[...], (CLS, SEQ))
        owner_m = jnp.sum(jnp.where(iota((CLS, SEQ), 1) == residue_m, perm, 0), axis=1, keepdims=True)
        d_at = MSG * owner_m + 8 + ((iota((CLS, 1), 0) & 31) >> 3)
        take_d = onehot(iota((CLS, SEQ * MSG), 1) == d_at)
        take_l = onehot(n_row == MSG * at_h + 12)
        tri = onehot(iota((SEQ, SEQ), 1) < iota((SEQ, SEQ), 0))
        starts = dot(tri, counts.astype(BF16)).astype(I32)
        base = (starts - cls + 7) >> 3
        after = (starts + counts - cls + 7) >> 3
        base2 = jnp.concatenate([base, base], axis=1)
        after2 = jnp.concatenate([after, after], axis=1)
        p_lane = iota((SEQ, CLS), 1)
        of_home = (base2 <= p_lane) & (p_lane < after2)
        lane_p = jnp.sum(jnp.where(of_home, p_lane - base2, 0), axis=0, keepdims=True)
        lanes = onehot(iota((128, CLS), 0) == lane_p)

        n_sub = iota((SEQ * MSG, SEQ), 0)
        rep = onehot((n_sub >> 4) == iota((SEQ * MSG, SEQ), 1))
        perm_o = jnp.broadcast_to(perm_ref[...], (SEQ, SEQ))
        res_o = jnp.sum(jnp.where(perm_o == iota((SEQ, SEQ), 0), iota((SEQ, SEQ), 1), 0), axis=1, keepdims=True)
        three = jnp.concatenate([base, after, jnp.broadcast_to(res_o, (SEQ, 128))], axis=1).astype(F32).astype(BF16)
        wide = dot(rep, three[:, :256]).astype(I32)
        t_col = iota((SEQ * MSG, 128), 0) & 15
        p_col = wide[:, :128] + (t_col & 7)
        live_col = p_col < wide[:, 128:256]
        lo_to = jnp.where(live_col & (t_col < 8), p_col, -1)
        hi_to = jnp.where(live_col & (t_col >= 8), p_col, -1)
        p_at = iota((SEQ * MSG, CLS), 1)
        put[0] = onehot(p_at == jnp.concatenate([lo_to, lo_to], axis=1))
        put[1] = onehot(p_at == jnp.concatenate([hi_to, hi_to], axis=1))
        rep_e = onehot((iota((SEQ * 8, SEQ), 0) >> 3) == iota((SEQ * 8, SEQ), 1))
        wide_e = dot(rep_e, three).astype(I32)
        t_e = iota((SEQ * 8, 128), 0) & 7
        e_col = wide_e[:, :128] + t_e
        e_to = jnp.where(e_col < wide_e[:, 128:256], e_col, -1)
        res_e = wide_e[:, 256:]
        o_to = jnp.where(t_e < 4, 32 * (res_e & 7) + 8 * t_e + (res_e >> 3), -1)
        put_e[0] = onehot(p_at[: SEQ * 8] == jnp.concatenate([e_to, e_to], axis=1))
        put_e[1] = onehot(p_at[: SEQ * 8] == jnp.concatenate([o_to, o_to], axis=1))
        put_g = onehot(iota((SEQ * 8, SEQ), 0) == 8 * iota((SEQ * 8, SEQ), 1) + 4)

        came(rows_b.at[pl.ds(0, SEQ - 1)], recv_sem.at[2])
        own_b.wait()
        b_rows = rows_b[...].reshape(SEQ * MSG, HD)
        dsend[...] = dot(take_d, b_rows).astype(BF16).reshape(WPH, 32, HD)

        def send_d(n, carry):
            to = lax.rem(cls + n, WPH)
            remote(dsend.at[to], dcls.at[cls], send_sem.at[6], recv_sem.at[3], {"seq": place_of(head, to)}).start()
            return carry

        lax.fori_loop(1, WPH, send_d, 0)
        dcls[cls] = dsend[cls]
        gone(dsend.at[pl.ds(0, WPH - 1)], 6)
        q = dot(take_lo, b_rows).astype(BF16)
        for n in (1, 3):
            pass_on(k_all, k_sem, 5, n)
        logit_h = dot(take_l, b_rows).astype(BF16)
        logit_p = jnp.sum(jnp.where(of_home, dot(logit_h, lanes), 0.0), axis=0, keepdims=True)
        gate = 1.0 / (1.0 + jnp.exp(-logit_p))

        top = jnp.full((1, CLS), -jnp.inf, F32)
        ahead = iota((CLS, CLS), 1) - iota((CLS, CLS), 0)
        order = ((0, 0), (0, 1), (1, 0), (3, 0), (1, 1), (3, 1), (2, 0), (2, 1))
        for n, flip in order:
            other = peer(n, flip)
            if (n, flip) == (1, 0):
                pass_on(k_all, k_sem, 5, 2)
            if flip:
                came(k_all.at[other], k_sem.at[other])
            later = jnp.where(other > cls, 1, 0)
            s = jnp.where(ahead >= later, dot_nt(k_all[other], q), -1e30)
            sbuf[2 * n + flip] = s
            top = jnp.maximum(top, jnp.max(s, axis=0, keepdims=True))
        gone(k_all.at[pl.ds(0, 3)], 5)
        for n in (1, 3):
            pass_on(v_all, v_sem, 7, n)
        total = jnp.zeros((1, CLS), F32)
        for n in range(WPH):
            e = jnp.exp2((sbuf[n] - top) * SCALE_LOG2)
            pbuf[n] = e.astype(BF16)
            total = total + jnp.sum(e, axis=0, keepdims=True)
        inv = 1.0 / total

        came(dcls.at[pl.ds(0, WPH - 1)], recv_sem.at[3])
        dy_t = dcls[...].reshape(CLS, HD).astype(F32).T
        dor_t = (dy_t * gate).astype(BF16).astype(F32)
        dor = (dor_t * inv).T.astype(BF16)

        def to_sibling(grads, part, pre, sems, sem, n):
            part[2 * n + 1] = grads.astype(BF16)
            remote(part.at[2 * n + 1], pre.at[n], send_sem.at[sem], sems.at[n], sibling).start()

        def to_class(grads, part, pre, pre_sems, total, sems, sem, n):
            came(pre.at[n], pre_sems.at[n])
            grads = grads + pre[n].astype(F32)
            if n:
                part[2 * n] = grads.astype(BF16)
                dst = {"seq": place_of(head, peer(n, 0))}
                remote(part.at[2 * n], total.at[x], send_sem.at[sem], sems.at[x], dst).start()
            return grads

        def collect(mine, total, sems):
            for n in (1, 3, 2):
                there = lax.rem(x + n, 4)
                came(total.at[there], sems.at[there])
                mine = mine + total[there].astype(F32)
            return mine.astype(BF16)

        far_first = (2, 1, 3, 0)
        for n in far_first:
            to_sibling(dot(pbuf[2 * n + 1], dor), part_v, pre_v, pre_v_sem, 9, n)
        gone(part_v.at[pl.ds(0, 4)], 9)
        pass_on(v_all, v_sem, 7, 2)
        gone(v_all.at[pl.ds(0, 3)], 7)
        out_t = jnp.zeros((HD, CLS), F32)
        for n, flip in order:
            other = peer(n, flip)
            if flip:
                came(v_all.at[other], v_sem.at[other])
            out_t = out_t + dot_tn(v_all[other], pbuf[2 * n + flip])
        out_t = out_t * inv
        delta = jnp.sum(dor_t * out_t, axis=0, keepdims=True) * inv
        gate_grad = jnp.sum(dy_t * out_t, axis=0, keepdims=True)
        gsend[...] = (out_t * gate).T.astype(BF16).reshape(WPH, 32, HD)

        def send_gated(n, carry):
            to = lax.rem(cls + n, WPH)
            remote(gsend.at[to], gchk.at[cls], send_sem.at[8], recv_sem.at[4], {"seq": place_of(head, to)}).start()
            return carry

        lax.fori_loop(1, WPH, send_gated, 0)
        gchk[cls] = gsend[cls]
        gone(gsend.at[pl.ds(0, WPH - 1)], 8)
        for n in far_first:
            mine_v = to_class(dot(pbuf[2 * n], dor), part_v, pre_v, pre_v_sem, sum_v, sum_v_sem, 10, n)
        gone(part_v.at[pl.ds(0, 3)], 10)
        dq_t = jnp.zeros((HD, CLS), F32)
        for flip in (1, 0):
            for n in far_first:
                other = peer(n, flip)
                dp = dot_nt(v_all[other], dor)
                ds = (pbuf[2 * n + flip].astype(F32) * (dp - delta)).astype(BF16)
                dq_t = dq_t + dot_tn(k_all[other], ds)
                if flip:
                    to_sibling(dot(ds, q) * SCALE, part_k, pre_k, pre_k_sem, 11, n)
                else:
                    pbuf[2 * n] = ds
        for n in far_first:
            mine_k = to_class(dot(pbuf[2 * n], q) * SCALE, part_k, pre_k, pre_k_sem, sum_k, sum_k_sem, 12, n)
        gone(part_k.at[pl.ds(0, 4)], 11)
        gone(part_k.at[pl.ds(0, 3)], 12)

        def send_back(back, home, sem, recv, own):
            def send_one(n, carry):
                to = lax.rem(me + n, SEQ)
                remote(back.at[to], home.at[slot], send_sem.at[sem], recv_sem.at[recv], {"seq": to}).start()
                return carry

            lax.fori_loop(1, SEQ, send_one, 0)
            gone(back.at[pl.ds(0, SEQ - 1)], sem)
            mine = pltpu.make_async_copy(back.at[me], home.at[slot], loc_sem.at[own])
            mine.start()
            return mine

        dqc = (dq_t * SCALE).T.astype(BF16)
        back_q[...] = dot(put_e[0], dqc).astype(BF16).reshape(SEQ, 8, HD)
        own_q = send_back(back_q, home_q, 14, 6, 1)
        gg_home = dot_nt(jnp.where(of_home, gate_grad, 0.0).astype(BF16), lanes).astype(BF16)
        came(gchk.at[pl.ds(0, WPH - 1)], recv_sem.at[4])
        full = dot(put_g, gg_home) + dot(put_e[1], gchk[...].reshape(CLS, HD))
        back_c[...] = full.astype(BF16).reshape(SEQ, 8, HD)
        own_c = send_back(back_c, home_c, 17, 9, 3)
        rest = dot(put[1], collect(mine_v, sum_v, sum_v_sem))
        full = dot(put[0], collect(mine_k, sum_k, sum_k_sem)) + rest
        back_b[...] = full.astype(BF16).reshape(SEQ, MSG, HD)
        own_b = send_back(back_b, home_b, 15, 7, 0)
        own_q.wait()
        own_c.wait()
        own_b.wait()
        came(home_c.at[pl.ds(0, workers - 1)], recv_sem.at[9])

    @pl.when(jnp.logical_not(is_worker))
    def _():
        came(home_c, recv_sem.at[9])

    keep_c = pltpu.make_async_copy(home_c, home_c_out, loc_sem.at[2])
    keep_c.start()
    gate_rows = jnp.zeros((CAP, HD), F32)
    take_g = onehot((iota((CAP, 128), 1) == 8 * ((start + iota((CAP, 128), 0)) & 7) + 4)[:, :CAP])
    for k in range(heads):
        gate_rows = gate_rows + dot(take_g, home_c[pl.ds(k * WPH, WPH)].reshape(WPH * 8, HD))
    mine_lane = iota((CAP, HD), 1) == (iota((CAP, HD), 0) >> 3)
    gate_grad = jnp.sum(jnp.where(mine_lane, gate_rows, 0.0), axis=1, keepdims=True)
    gg[tp] = jnp.broadcast_to(gate_grad, (CAP, 128))
    for n in range(1, n_tp):
        remote(gg.at[tp], gg.at[tp], send_sem.at[13], recv_sem.at[5], {"tp": lax.rem(tp + n, n_tp)}).start()

    @pl.when(is_worker)
    def _():
        done()
        came(home_q.at[pl.ds(0, workers - 1)], recv_sem.at[6])
        came(home_b.at[pl.ds(0, workers - 1)], recv_sem.at[7])

    @pl.when(jnp.logical_not(is_worker))
    def _():
        remote(msg_k, msg_k, send_sem.at[1], recv_sem.at[1], sibling).wait_send()
        remote(msg_v, msg_v, send_sem.at[16], recv_sem.at[8], sibling).wait_send()
        remote(msg_b, msg_b, send_sem.at[2], recv_sem.at[2], sibling).wait_send()
        came(home_q, recv_sem.at[6])
        came(home_b, recv_sem.at[7])

    if n_tp > 1:
        others = gg.at[pl.ds(0, n_tp - 1)]
        remote(others, others, send_sem.at[13], recv_sem.at[5], sibling).wait()
    gate_ref[...] = jnp.sum(gg[...], axis=0)
    keep_c.wait()
    remote(counted, counted, send_sem.at[0], recv_sem.at[0], sibling).wait_send()


def finish(
    heads, picked_ref, logit_ref, start_ref, gate_ref, home_c, home_q, home_b, gated_ref, dq_ref, dk_ref, dv_ref, router_ref
):
    me = lax.axis_index("seq")
    start = start_ref[...]
    spots, logit_col = find_logits(me, picked_ref[...], logit_ref[...])
    gate_col = 1.0 / (1.0 + jnp.exp(-logit_col))
    col = iota((CAP, 128), 1)
    j = iota((CAP, 128), 0)
    from_cls = MSG * ((start + j) & 7)
    lo = from_cls + (j >> 3)
    take_lo = col == lo
    take_e = onehot((col == 8 * ((start + j) & 7) + (j >> 3))[:, :CAP])
    take_o = onehot(((col == 8 * (j >> 2) + (j & 3)) & (j < 32))[:32, :CAP])
    take_b = jnp.concatenate([onehot(take_lo), onehot(col == lo + 8)], axis=0)
    for k in range(heads):
        cols = slice(k * HD, (k + 1) * HD)
        dq_ref[:, cols] = dot(take_e, home_q[pl.ds(k * WPH, WPH)].reshape(WPH * 8, HD)).astype(BF16)
        gated_ref[:, cols] = dot(take_o, home_c[pl.ds(k * WPH, WPH)].reshape(WPH * 8, HD)).astype(BF16)
        res = dot(take_b, home_b[pl.ds(k * WPH, WPH)].reshape(WPH * MSG, HD))
        dk_ref[:, cols] = res[0:64].astype(BF16)
        dv_ref[:, cols] = res[64:128].astype(BF16)
    gate_grad = gate_ref[...][:, 0:1]
    logit_grad = gate_grad * gate_col * (1.0 - gate_col)
    router_ref[...] = jnp.sum(jnp.where(spots, jnp.broadcast_to(logit_grad, (CAP, TOK)), 0.0), axis=0, keepdims=True)


def body(picked, owner_perm, router_logit, queries, keys, values, out_grad):
    n_tp = lax.axis_size("tp")
    heads = queries.shape[1] // HD
    width = heads * HD
    workers = heads * WPH
    picks = out_grad.shape[0]
    vmem = pl.BlockSpec(memory_space=pltpu.VMEM)
    hbm = pl.BlockSpec(memory_space=pltpu.HBM)
    dma = pltpu.SemaphoreType.DMA
    picked = picked.reshape(1, CAP)
    router_logit = router_logit.reshape(2, TOK // 2)
    start, gate_grad, home_c, home_q, home_b = pl.pallas_call(
        functools.partial(kernel, n_tp, heads),
        out_shape=(
            jax.ShapeDtypeStruct((1, 128), I32),
            jax.ShapeDtypeStruct((CAP, 128), F32),
            jax.ShapeDtypeStruct((workers, 8, HD), BF16),
            jax.ShapeDtypeStruct((workers, 8, HD), BF16),
            jax.ShapeDtypeStruct((workers, MSG, HD), BF16),
        ),
        in_specs=[hbm] * 7,
        out_specs=[vmem, vmem, hbm, hbm, hbm],
        scratch_shapes=[
            pltpu.VMEM((1, CAP), I32),
            pltpu.VMEM((1, SEQ), I32),
            pltpu.VMEM((2, TOK // 2), BF16),
            pltpu.VMEM((CAP, width), BF16),
            pltpu.VMEM((CAP, width), BF16),
            pltpu.VMEM((CAP, width), BF16),
            pltpu.VMEM((picks, width), BF16),
            pltpu.VMEM((1, 128), I32),
            pltpu.VMEM((SEQ, 1, 128), I32),
            pltpu.VMEM((workers, 8, HD), BF16),
            pltpu.VMEM((workers, 8, HD), BF16),
            pltpu.VMEM((workers, MSG, HD), BF16),
            pltpu.VMEM((SEQ, 8, HD), BF16),
            pltpu.VMEM((SEQ, 8, HD), BF16),
            pltpu.VMEM((SEQ, MSG, HD), BF16),
            pltpu.VMEM((WPH, CLS, HD), BF16),
            pltpu.VMEM((WPH, CLS, HD), BF16),
            pltpu.VMEM((WPH, 32, HD), BF16),
            pltpu.VMEM((WPH, 32, HD), BF16),
            pltpu.VMEM((2, SEQ * MSG, CLS), BF16),
            pltpu.VMEM((2, SEQ * 8, CLS), BF16),
            pltpu.VMEM((WPH, CLS, CLS), F32),
            pltpu.VMEM((WPH, CLS, CLS), BF16),
            pltpu.VMEM((WPH, CLS, HD), BF16),
            pltpu.VMEM((WPH, CLS, HD), BF16),
            pltpu.VMEM((4, CLS, HD), BF16),
            pltpu.VMEM((4, CLS, HD), BF16),
            pltpu.VMEM((4, CLS, HD), BF16),
            pltpu.VMEM((4, CLS, HD), BF16),
            pltpu.VMEM((WPH, 32, HD), BF16),
            pltpu.VMEM((WPH, 32, HD), BF16),
            pltpu.VMEM((n_tp, CAP, 128), F32),
            pltpu.VMEM((SEQ, 8, HD), BF16),
            pltpu.VMEM((SEQ, 8, HD), BF16),
            pltpu.VMEM((SEQ, MSG, HD), BF16),
            pltpu.VMEM((workers, 8, HD), BF16),
            dma((7,)),
            dma((18,)),
            dma((10,)),
            dma((WPH,)),
            dma((WPH,)),
            dma((4,)),
            dma((4,)),
            dma((4,)),
            dma((4,)),
            dma((4,)),
        ],
        compiler_params=pltpu.CompilerParams(
            collective_id=0, has_side_effects=True, vmem_limit_bytes=60 * 1024 * 1024
        ),
    )(
        picked,
        owner_perm.reshape(1, SEQ),
        router_logit,
        queries,
        keys,
        values,
        out_grad,
    )
    gated, dq, dk, dv, router = pl.pallas_call(
        functools.partial(finish, heads),
        out_shape=(
            jax.ShapeDtypeStruct((picks, width), BF16),
            jax.ShapeDtypeStruct((CAP, width), BF16),
            jax.ShapeDtypeStruct((CAP, width), BF16),
            jax.ShapeDtypeStruct((CAP, width), BF16),
            jax.ShapeDtypeStruct((1, TOK), F32),
        ),
        in_specs=[vmem] * 7,
        out_specs=[vmem] * 5,
        compiler_params=pltpu.CompilerParams(vmem_limit_bytes=60 * 1024 * 1024),
    )(picked, router_logit, start, gate_grad, home_c, home_q, home_b)
    return gated, dq, dk, dv, router.reshape(TOK)


def solution(mesh):
    return jax.shard_map(
        body,
        mesh=mesh,
        in_specs=(P("seq"), P(), P("seq"), P("seq", "tp"), P("seq", "tp"), P("seq", "tp"), P("seq", "tp")),
        out_specs=(P("seq", "tp"), P("seq", "tp"), P("seq", "tp"), P("seq", "tp"), P("seq")),
        check_vma=False,
    )
```

```python
import functools

import jax
import jax.numpy as jnp
from jax import lax
from jax.experimental import pallas as pl
from jax.experimental.pallas import tpu as pltpu
from jax.sharding import PartitionSpec as P

HD = 128
SEQ = 64
CAP = 64
TOK = 256
WPH = 8
CLS = 256
MSG = 16
SCALE = HD ** -0.5
SCALE_LOG2 = SCALE * 1.4426950408889634
MESH = pl.DeviceIdType.MESH
BF16, F32, I32 = jnp.bfloat16, jnp.float32, jnp.int32


def iota(shape, axis):
    return lax.broadcasted_iota(I32, shape, axis)


def onehot(hit):
    return jnp.where(hit, 1.0, 0.0).astype(BF16)


def dot(a, b):
    return lax.dot_general(a, b, (((1,), (0,)), ((), ())), preferred_element_type=F32)


def dot_nt(a, b):
    return lax.dot_general(a, b, (((1,), (1,)), ((), ())), preferred_element_type=F32)


def dot_tn(a, b):
    return lax.dot_general(a, b, (((0,), (0,)), ((), ())), preferred_element_type=F32)


def place_of(head, cls):
    z = head + head // 3
    return (cls // 2) * 16 + z * 2 + lax.rem(cls, 2)


def remote(src, dst, send, recv, device):
    return pltpu.make_async_remote_copy(
        src_ref=src, dst_ref=dst, send_sem=send, recv_sem=recv, device_id=device, device_id_type=MESH
    )


def find_logits(me, picked, logits):
    eye = iota((CAP, CAP), 0) == iota((CAP, CAP), 1)
    picked_col = jnp.sum(jnp.where(eye, jnp.broadcast_to(picked, (CAP, CAP)), 0), axis=1, keepdims=True)
    spots = jnp.broadcast_to(picked_col - me * TOK, (CAP, TOK)) == iota((CAP, TOK), 1)
    halves = logits.astype(F32)
    wide = jnp.broadcast_to(jnp.concatenate([halves[0:1], halves[1:2]], axis=1), (CAP, TOK))
    return spots, jnp.sum(jnp.where(spots, wide, 0.0), axis=1, keepdims=True)


def kernel(
    n_tp,
    heads,
    picked_in,
    perm_in,
    logit_in,
    q_in,
    k_in,
    v_in,
    d_in,
    start_ref,
    gate_ref,
    home_c_out,
    home_q,
    home_b,
    picked_ref,
    perm_ref,
    logit_ref,
    q_ref,
    k_ref,
    v_ref,
    d_ref,
    cnt_out,
    cnt,
    msg_k,
    msg_v,
    msg_b,
    rows_k,
    rows_v,
    rows_b,
    k_all,
    v_all,
    dsend,
    dcls,
    put,
    put_e,
    sbuf,
    pbuf,
    part_k,
    part_v,
    pre_k,
    pre_v,
    sum_k,
    sum_v,
    gsend,
    gchk,
    gg,
    back_q,
    back_c,
    back_b,
    home_c,
    in_sem,
    send_sem,
    recv_sem,
    k_sem,
    v_sem,
    pre_k_sem,
    pre_v_sem,
    sum_k_sem,
    sum_v_sem,
    loc_sem,
):
    me = lax.axis_index("seq")
    tp = lax.axis_index("tp")
    z = lax.rem(lax.div(me, 2), 8)
    core = lax.rem(me, 2)
    x = lax.div(me, 16)
    is_worker = lax.rem(z, 4) < 3
    head = z - lax.div(z, 4)
    cls = x * 2 + core
    slot = head * WPH + cls
    workers = heads * WPH
    sibling = {"seq": me + 1 - 2 * core}

    loads = [
        pltpu.make_async_copy(src, dst, in_sem.at[n])
        for n, (src, dst) in enumerate(
            zip(
                (picked_in, perm_in, logit_in, k_in, v_in, q_in, d_in),
                (picked_ref, perm_ref, logit_ref, k_ref, v_ref, q_ref, d_ref),
            )
        )
    ]
    for load in loads:
        load.start()

    barrier = pltpu.get_barrier_semaphore()

    def greet(n, carry):
        pl.semaphore_signal(barrier, inc=1, device_id={"seq": lax.rem(me + n, SEQ)}, device_id_type=MESH)
        return carry

    lax.fori_loop(1, SEQ, greet, 0, unroll=7)
    for n in range(1, n_tp):
        pl.semaphore_signal(barrier, inc=1, device_id={"tp": lax.rem(tp + n, n_tp)}, device_id_type=MESH)

    loads[0].wait()
    picked = picked_ref[...]
    count = jnp.sum(jnp.where(picked >= 0, 1, 0), axis=1, keepdims=True)
    cnt_out[...] = jnp.broadcast_to(count, (1, 128))
    pl.semaphore_wait(barrier, SEQ - 1 + n_tp - 1)

    def send_count(n, carry):
        remote(cnt_out, cnt.at[me], send_sem.at[0], recv_sem.at[0], {"seq": lax.rem(me + n, SEQ)}).start()
        return carry

    lax.fori_loop(1, SEQ, send_count, 0, unroll=7)
    cnt[me] = cnt_out[...]

    for load in loads[1:]:
        load.wait()
    spots, logit_col = find_logits(me, picked, logit_ref[...])
    spread = jnp.where(iota((CAP, 128), 1) == (iota((CAP, 128), 0) >> 3), jnp.broadcast_to(logit_col, (CAP, 128)), 0.0)
    spread = spread.astype(BF16)
    fill = jnp.zeros((32, HD), BF16)

    counted = cnt.at[pl.ds(0, SEQ - 1)]
    remote(counted, counted, send_sem.at[0], recv_sem.at[0], sibling).wait_recv()
    counts = jnp.sum(cnt[...], axis=1)
    start = jnp.sum(jnp.where(iota((SEQ, 128), 0) < me, counts, 0), axis=0, keepdims=True)
    start_ref[...] = start

    n_half = iota((WPH * 8, CAP), 0)
    turn_half = ((n_half >> 3) - start[:, :CAP]) & 7
    pick_half = onehot(iota((WPH * 8, CAP), 1) == 8 * (n_half & 7) + turn_half)
    n_out = iota((WPH * MSG, 128), 0)
    t_out = n_out & 15
    turn = ((n_out >> 4) - start) & 7
    src = iota((WPH * MSG, 128), 1)
    b_from = jnp.where(t_out < 8, 8 * t_out + turn, jnp.where(t_out < 12, CAP + 4 * (n_out >> 4) + t_out - 8, -1))
    pick_b = onehot(src == b_from)
    src64 = iota((WPH * MSG, CAP), 1)
    pick_logit = onehot((t_out[:, :CAP] == 12) & ((src64 & 7) == turn[:, :CAP]))

    def send_rows(msg, rows, sem, recv):
        def send_one(n, carry):
            w = lax.rem(n + me, workers)
            dst = place_of(lax.div(w, WPH), lax.rem(w, WPH))

            @pl.when(dst != me)
            def _():
                remote(msg.at[w], rows.at[me], send_sem.at[sem], recv_sem.at[recv], {"seq": dst}).start()

            return carry

        lax.fori_loop(0, workers, send_one, 0, unroll=6)

    for ref, msg, rows, sem, recv in ((k_ref, msg_k, rows_k, 1, 1), (v_ref, msg_v, rows_v, 16, 8)):
        turned = dot(pick_half, ref[...]).astype(BF16)
        for k in range(heads):
            msg[pl.ds(k * WPH, WPH)] = turned[:, k * HD : (k + 1) * HD].reshape(WPH, 8, HD)
        send_rows(msg, rows, sem, recv)
    logit_rows = dot(pick_logit, spread)
    for k in range(heads):
        cols = slice(k * HD, (k + 1) * HD)
        both = dot(pick_b, jnp.concatenate([q_ref[:, cols], d_ref[:, cols], fill], axis=0)) + logit_rows
        msg_b[pl.ds(k * WPH, WPH)] = both.astype(BF16).reshape(WPH, MSG, HD)
    send_rows(msg_b, rows_b, 2, 2)
    left = []

    def gone(src, sem):
        left.append((src, sem))

    def done():
        for src, sem in left:
            remote(src, src, send_sem.at[sem], recv_sem.at[0], sibling).wait_send()

    def came(ref, sem):
        remote(ref, ref, send_sem.at[0], sem, sibling).wait_recv()

    @pl.when(is_worker)
    def _():
        own_k = pltpu.make_async_copy(msg_k.at[slot], rows_k.at[me], loc_sem.at[0])
        own_k.start()
        own_v = pltpu.make_async_copy(msg_v.at[slot], rows_v.at[me], loc_sem.at[3])
        own_v.start()
        own_b = pltpu.make_async_copy(msg_b.at[slot], rows_b.at[me], loc_sem.at[1])
        own_b.start()
        gone(msg_k.at[pl.ds(0, workers - 1)], 1)
        gone(msg_v.at[pl.ds(0, workers - 1)], 16)
        gone(msg_b.at[pl.ds(0, workers - 1)], 2)

        def peer(n, flip):
            return lax.rem(x + n, 4) * 2 + (1 - core if flip else core)

        def send_all(ref, sems, sem):
            remote(ref.at[cls], ref.at[cls], send_sem.at[sem], sems.at[cls], sibling).start()
            for n in (1, 3, 2):
                dst = {"seq": place_of(head, peer(n, 0))}
                remote(ref.at[cls], ref.at[cls], send_sem.at[sem], sems.at[cls], dst).start()
            gone(ref.at[pl.ds(0, 4)], sem)

        def pass_on(ref, sems, sem, n):
            block = ref.at[peer(n, 0)]
            came(block, sems.at[peer(n, 0)])
            remote(block, block, send_sem.at[sem], sems.at[peer(n, 0)], sibling).start()

        n_row = iota((SEQ, SEQ * MSG), 1)
        below = jnp.concatenate([counts] * 8, axis=1)
        at_h = iota((SEQ, SEQ * MSG), 0)
        start_n = jnp.sum(jnp.where(at_h < (n_row >> 4), below, 0), axis=0, keepdims=True)
        end_n = jnp.sum(jnp.where(at_h <= (n_row >> 4), below, 0), axis=0, keepdims=True)
        t_n = iota((1, SEQ * MSG), 1) & 15
        p_n = ((start_n - cls + 7) >> 3) + (t_n & 7)
        live_n = p_n < ((end_n - cls + 7) >> 3)
        lo_at = jnp.where(live_n & (t_n < 8), p_n, -1)
        p_sub = iota((CLS, SEQ * MSG), 0)
        take_lo = onehot(p_sub == lo_at)

        n_eight = iota((SEQ, SEQ * 8), 1)
        start_e = jnp.sum(jnp.where(at_h[:, : SEQ * 8] < (n_eight >> 3), below[:, : SEQ * 8], 0), axis=0, keepdims=True)
        end_e = jnp.sum(jnp.where(at_h[:, : SEQ * 8] <= (n_eight >> 3), below[:, : SEQ * 8], 0), axis=0, keepdims=True)
        p_e = ((start_e - cls + 7) >> 3) + (n_eight[0:1] & 7)
        e_at = jnp.where(p_e < ((end_e - cls + 7) >> 3), p_e, -1)
        take_eight = onehot(p_sub[:, : SEQ * 8] == e_at)

        came(rows_k.at[pl.ds(0, SEQ - 1)], recv_sem.at[1])
        own_k.wait()
        k_all[cls] = dot(take_eight, rows_k[...].reshape(SEQ * 8, HD)).astype(BF16)
        send_all(k_all, k_sem, 3)
        came(rows_v.at[pl.ds(0, SEQ - 1)], recv_sem.at[8])
        own_v.wait()
        v_all[cls] = dot(take_eight, rows_v[...].reshape(SEQ * 8, HD)).astype(BF16)
        send_all(v_all, v_sem, 4)

        m_sub = iota((CLS, SEQ), 0)
        residue_m = 8 * (m_sub & 7) + (m_sub >> 5)
        perm = jnp.broadcast_to(perm_ref[...], (CLS, SEQ))
        owner_m = jnp.sum(jnp.where(iota((CLS, SEQ), 1) == residue_m, perm, 0), axis=1, keepdims=True)
        d_at = MSG * owner_m + 8 + ((iota((CLS, 1), 0) & 31) >> 3)
        take_d = onehot(iota((CLS, SEQ * MSG), 1) == d_at)
        take_l = onehot(n_row == MSG * at_h + 12)
        tri = onehot(iota((SEQ, SEQ), 1) < iota((SEQ, SEQ), 0))
        starts = dot(tri, counts.astype(BF16)).astype(I32)
        base = (starts - cls + 7) >> 3
        after = (starts + counts - cls + 7) >> 3
        base2 = jnp.concatenate([base, base], axis=1)
        after2 = jnp.concatenate([after, after], axis=1)
        p_lane = iota((SEQ, CLS), 1)
        of_home = (base2 <= p_lane) & (p_lane < after2)
        lane_p = jnp.sum(jnp.where(of_home, p_lane - base2, 0), axis=0, keepdims=True)
        lanes = onehot(iota((128, CLS), 0) == lane_p)

        n_sub = iota((SEQ * MSG, SEQ), 0)
        rep = onehot((n_sub >> 4) == iota((SEQ * MSG, SEQ), 1))
        perm_o = jnp.broadcast_to(perm_ref[...], (SEQ, SEQ))
        res_o = jnp.sum(jnp.where(perm_o == iota((SEQ, SEQ), 0), iota((SEQ, SEQ), 1), 0), axis=1, keepdims=True)
        three = jnp.concatenate([base, after, jnp.broadcast_to(res_o, (SEQ, 128))], axis=1).astype(F32).astype(BF16)
        wide = dot(rep, three[:, :256]).astype(I32)
        t_col = iota((SEQ * MSG, 128), 0) & 15
        p_col = wide[:, :128] + (t_col & 7)
        live_col = p_col < wide[:, 128:256]
        lo_to = jnp.where(live_col & (t_col < 8), p_col, -1)
        hi_to = jnp.where(live_col & (t_col >= 8), p_col, -1)
        p_at = iota((SEQ * MSG, CLS), 1)
        put[0] = onehot(p_at == jnp.concatenate([lo_to, lo_to], axis=1))
        put[1] = onehot(p_at == jnp.concatenate([hi_to, hi_to], axis=1))
        rep_e = onehot((iota((SEQ * 8, SEQ), 0) >> 3) == iota((SEQ * 8, SEQ), 1))
        wide_e = dot(rep_e, three).astype(I32)
        t_e = iota((SEQ * 8, 128), 0) & 7
        e_col = wide_e[:, :128] + t_e
        e_to = jnp.where(e_col < wide_e[:, 128:256], e_col, -1)
        res_e = wide_e[:, 256:]
        o_to = jnp.where(t_e < 4, 32 * (res_e & 7) + 8 * t_e + (res_e >> 3), -1)
        put_e[0] = onehot(p_at[: SEQ * 8] == jnp.concatenate([e_to, e_to], axis=1))
        put_e[1] = onehot(p_at[: SEQ * 8] == jnp.concatenate([o_to, o_to], axis=1))
        put_g = onehot(iota((SEQ * 8, SEQ), 0) == 8 * iota((SEQ * 8, SEQ), 1) + 4)

        came(rows_b.at[pl.ds(0, SEQ - 1)], recv_sem.at[2])
        own_b.wait()
        b_rows = rows_b[...].reshape(SEQ * MSG, HD)
        dsend[...] = dot(take_d, b_rows).astype(BF16).reshape(WPH, 32, HD)

        def send_d(n, carry):
            to = lax.rem(cls + n, WPH)
            remote(dsend.at[to], dcls.at[cls], send_sem.at[6], recv_sem.at[3], {"seq": place_of(head, to)}).start()
            return carry

        lax.fori_loop(1, WPH, send_d, 0)
        dcls[cls] = dsend[cls]
        gone(dsend.at[pl.ds(0, WPH - 1)], 6)
        q = dot(take_lo, b_rows).astype(BF16)
        for n in (1, 3):
            pass_on(k_all, k_sem, 5, n)
        logit_h = dot(take_l, b_rows).astype(BF16)
        logit_p = jnp.sum(jnp.where(of_home, dot(logit_h, lanes), 0.0), axis=0, keepdims=True)
        gate = 1.0 / (1.0 + jnp.exp(-logit_p))

        top = jnp.full((1, CLS), -jnp.inf, F32)
        ahead = iota((CLS, CLS), 1) - iota((CLS, CLS), 0)
        order = ((0, 0), (0, 1), (1, 0), (3, 0), (1, 1), (3, 1), (2, 0), (2, 1))
        for n, flip in order:
            other = peer(n, flip)
            if (n, flip) == (1, 0):
                pass_on(k_all, k_sem, 5, 2)
            if flip:
                came(k_all.at[other], k_sem.at[other])
            later = jnp.where(other > cls, 1, 0)
            s = jnp.where(ahead >= later, dot_nt(k_all[other], q), -1e30)
            sbuf[2 * n + flip] = s
            top = jnp.maximum(top, jnp.max(s, axis=0, keepdims=True))
        gone(k_all.at[pl.ds(0, 3)], 5)
        for n in (1, 3):
            pass_on(v_all, v_sem, 7, n)
        total = jnp.zeros((1, CLS), F32)
        for n in range(WPH):
            e = jnp.exp2((sbuf[n] - top) * SCALE_LOG2)
            pbuf[n] = e.astype(BF16)
            total = total + jnp.sum(e, axis=0, keepdims=True)
        inv = 1.0 / total

        came(dcls.at[pl.ds(0, WPH - 1)], recv_sem.at[3])
        dy_t = dcls[...].reshape(CLS, HD).astype(F32).T
        dor_t = (dy_t * gate).astype(BF16).astype(F32)
        dor = (dor_t * inv).T.astype(BF16)

        def to_sibling(grads, part, pre, sems, sem, n):
            part[2 * n + 1] = grads.astype(BF16)
            remote(part.at[2 * n + 1], pre.at[n], send_sem.at[sem], sems.at[n], sibling).start()

        def to_class(grads, part, pre, pre_sems, total, sems, sem, n):
            came(pre.at[n], pre_sems.at[n])
            grads = grads + pre[n].astype(F32)
            if n:
                part[2 * n] = grads.astype(BF16)
                dst = {"seq": place_of(head, peer(n, 0))}
                remote(part.at[2 * n], total.at[x], send_sem.at[sem], sems.at[x], dst).start()
            return grads

        def collect(mine, total, sems):
            for n in (1, 3, 2):
                there = lax.rem(x + n, 4)
                came(total.at[there], sems.at[there])
                mine = mine + total[there].astype(F32)
            return mine.astype(BF16)

        far_first = (2, 1, 3, 0)
        for n in far_first:
            to_sibling(dot(pbuf[2 * n + 1], dor), part_v, pre_v, pre_v_sem, 9, n)
        gone(part_v.at[pl.ds(0, 4)], 9)
        pass_on(v_all, v_sem, 7, 2)
        for n in far_first:
            mine_v = to_class(dot(pbuf[2 * n], dor), part_v, pre_v, pre_v_sem, sum_v, sum_v_sem, 10, n)
        gone(part_v.at[pl.ds(0, 3)], 10)
        gone(v_all.at[pl.ds(0, 3)], 7)
        out_t = jnp.zeros((HD, CLS), F32)
        for n, flip in order:
            other = peer(n, flip)
            if flip:
                came(v_all.at[other], v_sem.at[other])
            out_t = out_t + dot_tn(v_all[other], pbuf[2 * n + flip])
        out_t = out_t * inv
        delta = jnp.sum(dor_t * out_t, axis=0, keepdims=True) * inv
        gate_grad = jnp.sum(dy_t * out_t, axis=0, keepdims=True)
        gsend[...] = (out_t * gate).T.astype(BF16).reshape(WPH, 32, HD)

        def send_gated(n, carry):
            to = lax.rem(cls + n, WPH)
            remote(gsend.at[to], gchk.at[cls], send_sem.at[8], recv_sem.at[4], {"seq": place_of(head, to)}).start()
            return carry

        lax.fori_loop(1, WPH, send_gated, 0)
        gchk[cls] = gsend[cls]
        gone(gsend.at[pl.ds(0, WPH - 1)], 8)
        dq_t = jnp.zeros((HD, CLS), F32)
        for flip in (1, 0):
            for n in far_first:
                other = peer(n, flip)
                dp = dot_nt(v_all[other], dor)
                ds = (pbuf[2 * n + flip].astype(F32) * (dp - delta)).astype(BF16)
                dq_t = dq_t + dot_tn(k_all[other], ds)
                if flip:
                    to_sibling(dot(ds, q) * SCALE, part_k, pre_k, pre_k_sem, 11, n)
                else:
                    pbuf[2 * n] = ds
        for n in far_first:
            mine_k = to_class(dot(pbuf[2 * n], q) * SCALE, part_k, pre_k, pre_k_sem, sum_k, sum_k_sem, 12, n)
        gone(part_k.at[pl.ds(0, 4)], 11)
        gone(part_k.at[pl.ds(0, 3)], 12)

        def send_back(back, home, sem, recv, own):
            def send_one(n, carry):
                to = lax.rem(me + n, SEQ)
                remote(back.at[to], home.at[slot], send_sem.at[sem], recv_sem.at[recv], {"seq": to}).start()
                return carry

            lax.fori_loop(1, SEQ, send_one, 0, unroll=7)
            gone(back.at[pl.ds(0, SEQ - 1)], sem)
            mine = pltpu.make_async_copy(back.at[me], home.at[slot], loc_sem.at[own])
            mine.start()
            return mine

        dqc = (dq_t * SCALE).T.astype(BF16)
        back_q[...] = dot(put_e[0], dqc).astype(BF16).reshape(SEQ, 8, HD)
        own_q = send_back(back_q, home_q, 14, 6, 1)
        gg_home = dot_nt(jnp.where(of_home, gate_grad, 0.0).astype(BF16), lanes).astype(BF16)
        came(gchk.at[pl.ds(0, WPH - 1)], recv_sem.at[4])
        full = dot(put_g, gg_home) + dot(put_e[1], gchk[...].reshape(CLS, HD))
        back_c[...] = full.astype(BF16).reshape(SEQ, 8, HD)
        own_c = send_back(back_c, home_c, 17, 9, 3)
        rest = dot(put[1], collect(mine_v, sum_v, sum_v_sem))
        full = dot(put[0], collect(mine_k, sum_k, sum_k_sem)) + rest
        back_b[...] = full.astype(BF16).reshape(SEQ, MSG, HD)
        own_b = send_back(back_b, home_b, 15, 7, 0)
        own_q.wait()
        own_c.wait()
        own_b.wait()
        came(home_c.at[pl.ds(0, workers - 1)], recv_sem.at[9])

    @pl.when(jnp.logical_not(is_worker))
    def _():
        came(home_c, recv_sem.at[9])

    keep_c = pltpu.make_async_copy(home_c, home_c_out, loc_sem.at[2])
    keep_c.start()
    gate_rows = jnp.zeros((CAP, HD), F32)
    take_g = onehot((iota((CAP, 128), 1) == 8 * ((start + iota((CAP, 128), 0)) & 7) + 4)[:, :CAP])
    for k in range(heads):
        gate_rows = gate_rows + dot(take_g, home_c[pl.ds(k * WPH, WPH)].reshape(WPH * 8, HD))
    mine_lane = iota((CAP, HD), 1) == (iota((CAP, HD), 0) >> 3)
    gate_grad = jnp.sum(jnp.where(mine_lane, gate_rows, 0.0), axis=1, keepdims=True)
    gg[tp] = jnp.broadcast_to(gate_grad, (CAP, 128))
    for n in range(1, n_tp):
        remote(gg.at[tp], gg.at[tp], send_sem.at[13], recv_sem.at[5], {"tp": lax.rem(tp + n, n_tp)}).start()

    @pl.when(is_worker)
    def _():
        done()
        came(home_q.at[pl.ds(0, workers - 1)], recv_sem.at[6])
        came(home_b.at[pl.ds(0, workers - 1)], recv_sem.at[7])

    @pl.when(jnp.logical_not(is_worker))
    def _():
        remote(msg_k, msg_k, send_sem.at[1], recv_sem.at[1], sibling).wait_send()
        remote(msg_v, msg_v, send_sem.at[16], recv_sem.at[8], sibling).wait_send()
        remote(msg_b, msg_b, send_sem.at[2], recv_sem.at[2], sibling).wait_send()
        came(home_q, recv_sem.at[6])
        came(home_b, recv_sem.at[7])

    if n_tp > 1:
        others = gg.at[pl.ds(0, n_tp - 1)]
        remote(others, others, send_sem.at[13], recv_sem.at[5], sibling).wait()
    gate_ref[...] = jnp.sum(gg[...], axis=0)
    keep_c.wait()
    remote(counted, counted, send_sem.at[0], recv_sem.at[0], sibling).wait_send()


def finish(
    heads, picked_ref, logit_ref, start_ref, gate_ref, home_c, home_q, home_b, gated_ref, dq_ref, dk_ref, dv_ref, router_ref
):
    me = lax.axis_index("seq")
    start = start_ref[...]
    spots, logit_col = find_logits(me, picked_ref[...], logit_ref[...])
    gate_col = 1.0 / (1.0 + jnp.exp(-logit_col))
    col = iota((CAP, 128), 1)
    j = iota((CAP, 128), 0)
    from_cls = MSG * ((start + j) & 7)
    lo = from_cls + (j >> 3)
    take_lo = col == lo
    take_e = onehot((col == 8 * ((start + j) & 7) + (j >> 3))[:, :CAP])
    take_o = onehot(((col == 8 * (j >> 2) + (j & 3)) & (j < 32))[:32, :CAP])
    take_b = jnp.concatenate([onehot(take_lo), onehot(col == lo + 8)], axis=0)
    for k in range(heads):
        cols = slice(k * HD, (k + 1) * HD)
        dq_ref[:, cols] = dot(take_e, home_q[pl.ds(k * WPH, WPH)].reshape(WPH * 8, HD)).astype(BF16)
        gated_ref[:, cols] = dot(take_o, home_c[pl.ds(k * WPH, WPH)].reshape(WPH * 8, HD)).astype(BF16)
        res = dot(take_b, home_b[pl.ds(k * WPH, WPH)].reshape(WPH * MSG, HD))
        dk_ref[:, cols] = res[0:64].astype(BF16)
        dv_ref[:, cols] = res[64:128].astype(BF16)
    gate_grad = gate_ref[...][:, 0:1]
    logit_grad = gate_grad * gate_col * (1.0 - gate_col)
    router_ref[...] = jnp.sum(jnp.where(spots, jnp.broadcast_to(logit_grad, (CAP, TOK)), 0.0), axis=0, keepdims=True)


def body(picked, owner_perm, router_logit, queries, keys, values, out_grad):
    n_tp = lax.axis_size("tp")
    heads = queries.shape[1] // HD
    width = heads * HD
    workers = heads * WPH
    picks = out_grad.shape[0]
    vmem = pl.BlockSpec(memory_space=pltpu.VMEM)
    hbm = pl.BlockSpec(memory_space=pltpu.HBM)
    dma = pltpu.SemaphoreType.DMA
    picked = picked.reshape(1, CAP)
    router_logit = router_logit.reshape(2, TOK // 2)
    start, gate_grad, home_c, home_q, home_b = pl.pallas_call(
        functools.partial(kernel, n_tp, heads),
        out_shape=(
            jax.ShapeDtypeStruct((1, 128), I32),
            jax.ShapeDtypeStruct((CAP, 128), F32),
            jax.ShapeDtypeStruct((workers, 8, HD), BF16),
            jax.ShapeDtypeStruct((workers, 8, HD), BF16),
            jax.ShapeDtypeStruct((workers, MSG, HD), BF16),
        ),
        in_specs=[hbm] * 7,
        out_specs=[vmem, vmem, hbm, hbm, hbm],
        scratch_shapes=[
            pltpu.VMEM((1, CAP), I32),
            pltpu.VMEM((1, SEQ), I32),
            pltpu.VMEM((2, TOK // 2), BF16),
            pltpu.VMEM((CAP, width), BF16),
            pltpu.VMEM((CAP, width), BF16),
            pltpu.VMEM((CAP, width), BF16),
            pltpu.VMEM((picks, width), BF16),
            pltpu.VMEM((1, 128), I32),
            pltpu.VMEM((SEQ, 1, 128), I32),
            pltpu.VMEM((workers, 8, HD), BF16),
            pltpu.VMEM((workers, 8, HD), BF16),
            pltpu.VMEM((workers, MSG, HD), BF16),
            pltpu.VMEM((SEQ, 8, HD), BF16),
            pltpu.VMEM((SEQ, 8, HD), BF16),
            pltpu.VMEM((SEQ, MSG, HD), BF16),
            pltpu.VMEM((WPH, CLS, HD), BF16),
            pltpu.VMEM((WPH, CLS, HD), BF16),
            pltpu.VMEM((WPH, 32, HD), BF16),
            pltpu.VMEM((WPH, 32, HD), BF16),
            pltpu.VMEM((2, SEQ * MSG, CLS), BF16),
            pltpu.VMEM((2, SEQ * 8, CLS), BF16),
            pltpu.VMEM((WPH, CLS, CLS), F32),
            pltpu.VMEM((WPH, CLS, CLS), BF16),
            pltpu.VMEM((WPH, CLS, HD), BF16),
            pltpu.VMEM((WPH, CLS, HD), BF16),
            pltpu.VMEM((4, CLS, HD), BF16),
            pltpu.VMEM((4, CLS, HD), BF16),
            pltpu.VMEM((4, CLS, HD), BF16),
            pltpu.VMEM((4, CLS, HD), BF16),
            pltpu.VMEM((WPH, 32, HD), BF16),
            pltpu.VMEM((WPH, 32, HD), BF16),
            pltpu.VMEM((n_tp, CAP, 128), F32),
            pltpu.VMEM((SEQ, 8, HD), BF16),
            pltpu.VMEM((SEQ, 8, HD), BF16),
            pltpu.VMEM((SEQ, MSG, HD), BF16),
            pltpu.VMEM((workers, 8, HD), BF16),
            dma((7,)),
            dma((18,)),
            dma((10,)),
            dma((WPH,)),
            dma((WPH,)),
            dma((4,)),
            dma((4,)),
            dma((4,)),
            dma((4,)),
            dma((4,)),
        ],
        compiler_params=pltpu.CompilerParams(
            collective_id=0, has_side_effects=True, vmem_limit_bytes=60 * 1024 * 1024
        ),
    )(
        picked,
        owner_perm.reshape(1, SEQ),
        router_logit,
        queries,
        keys,
        values,
        out_grad,
    )
    gated, dq, dk, dv, router = pl.pallas_call(
        functools.partial(finish, heads),
        out_shape=(
            jax.ShapeDtypeStruct((picks, width), BF16),
            jax.ShapeDtypeStruct((CAP, width), BF16),
            jax.ShapeDtypeStruct((CAP, width), BF16),
            jax.ShapeDtypeStruct((CAP, width), BF16),
            jax.ShapeDtypeStruct((1, TOK), F32),
        ),
        in_specs=[vmem] * 7,
        out_specs=[vmem] * 5,
        compiler_params=pltpu.CompilerParams(vmem_limit_bytes=60 * 1024 * 1024),
    )(picked, router_logit, start, gate_grad, home_c, home_q, home_b)
    return gated, dq, dk, dv, router.reshape(TOK)


def solution(mesh):
    return jax.shard_map(
        body,
        mesh=mesh,
        in_specs=(P("seq"), P(), P("seq"), P("seq", "tp"), P("seq", "tp"), P("seq", "tp"), P("seq", "tp")),
        out_specs=(P("seq", "tp"), P("seq", "tp"), P("seq", "tp"), P("seq", "tp"), P("seq")),
        check_vma=False,
    )
```

```python
import functools

import jax
import jax.numpy as jnp
from jax import lax
from jax.experimental import pallas as pl
from jax.experimental.pallas import tpu as pltpu
from jax.sharding import PartitionSpec as P

HD = 128
SEQ = 64
CAP = 64
TOK = 256
WPH = 8
CLS = 256
MSG = 16
SCALE = HD ** -0.5
SCALE_LOG2 = SCALE * 1.4426950408889634
MESH = pl.DeviceIdType.MESH
BF16, F32, I32 = jnp.bfloat16, jnp.float32, jnp.int32


def iota(shape, axis):
    return lax.broadcasted_iota(I32, shape, axis)


def onehot(hit):
    return jnp.where(hit, 1.0, 0.0).astype(BF16)


def dot(a, b):
    return lax.dot_general(a, b, (((1,), (0,)), ((), ())), preferred_element_type=F32)


def dot_nt(a, b):
    return lax.dot_general(a, b, (((1,), (1,)), ((), ())), preferred_element_type=F32)


def dot_tn(a, b):
    return lax.dot_general(a, b, (((0,), (0,)), ((), ())), preferred_element_type=F32)


def place_of(head, cls):
    z = head + head // 3
    return (cls // 2) * 16 + z * 2 + lax.rem(cls, 2)


def remote(src, dst, send, recv, device):
    return pltpu.make_async_remote_copy(
        src_ref=src, dst_ref=dst, send_sem=send, recv_sem=recv, device_id=device, device_id_type=MESH
    )


def find_logits(me, picked, logits):
    eye = iota((CAP, CAP), 0) == iota((CAP, CAP), 1)
    picked_col = jnp.sum(jnp.where(eye, jnp.broadcast_to(picked, (CAP, CAP)), 0), axis=1, keepdims=True)
    spots = jnp.broadcast_to(picked_col - me * TOK, (CAP, TOK)) == iota((CAP, TOK), 1)
    halves = logits.astype(F32)
    wide = jnp.broadcast_to(jnp.concatenate([halves[0:1], halves[1:2]], axis=1), (CAP, TOK))
    return spots, jnp.sum(jnp.where(spots, wide, 0.0), axis=1, keepdims=True)


def kernel(
    n_tp,
    heads,
    picked_in,
    perm_in,
    logit_in,
    q_in,
    k_in,
    v_in,
    d_in,
    start_ref,
    row_ref,
    home_c_out,
    home_q,
    home_b,
    picked_ref,
    perm_ref,
    logit_ref,
    q_ref,
    k_ref,
    v_ref,
    d_ref,
    cnt_out,
    cnt,
    msg_k,
    msg_v,
    msg_b,
    rows_k,
    rows_v,
    rows_b,
    k_all,
    v_all,
    dsend,
    dcls,
    put,
    put_e,
    sbuf,
    pbuf,
    part_k,
    part_v,
    pre_k,
    pre_v,
    sum_k,
    sum_v,
    gsend,
    gchk,
    gg,
    back_q,
    back_c,
    back_b,
    home_c,
    in_sem,
    send_sem,
    recv_sem,
    k_sem,
    v_sem,
    pre_k_sem,
    pre_v_sem,
    sum_k_sem,
    sum_v_sem,
    loc_sem,
):
    me = lax.axis_index("seq")
    tp = lax.axis_index("tp")
    z = lax.rem(lax.div(me, 2), 8)
    core = lax.rem(me, 2)
    x = lax.div(me, 16)
    is_worker = lax.rem(z, 4) < 3
    head = z - lax.div(z, 4)
    cls = x * 2 + core
    slot = head * WPH + cls
    workers = heads * WPH
    sibling = {"seq": me + 1 - 2 * core}

    loads = [
        pltpu.make_async_copy(src, dst, in_sem.at[n])
        for n, (src, dst) in enumerate(
            zip(
                (picked_in, perm_in, logit_in, k_in, v_in, q_in, d_in),
                (picked_ref, perm_ref, logit_ref, k_ref, v_ref, q_ref, d_ref),
            )
        )
    ]
    for load in loads:
        load.start()

    barrier = pltpu.get_barrier_semaphore()

    def greet(n, carry):
        pl.semaphore_signal(barrier, inc=1, device_id={"seq": lax.rem(me + n, SEQ)}, device_id_type=MESH)
        return carry

    lax.fori_loop(1, SEQ, greet, 0, unroll=7)
    for n in range(1, n_tp):
        pl.semaphore_signal(barrier, inc=1, device_id={"tp": lax.rem(tp + n, n_tp)}, device_id_type=MESH)

    loads[0].wait()
    picked = picked_ref[...]
    count = jnp.sum(jnp.where(picked >= 0, 1, 0), axis=1, keepdims=True)
    cnt_out[...] = jnp.broadcast_to(count, (1, 128))
    pl.semaphore_wait(barrier, SEQ - 1 + n_tp - 1)

    def send_count(n, carry):
        remote(cnt_out, cnt.at[me], send_sem.at[0], recv_sem.at[0], {"seq": lax.rem(me + n, SEQ)}).start()
        return carry

    lax.fori_loop(1, SEQ, send_count, 0, unroll=7)
    cnt[me] = cnt_out[...]

    for load in loads[1:]:
        load.wait()
    spots, logit_col = find_logits(me, picked, logit_ref[...])
    spread = jnp.where(iota((CAP, 128), 1) == (iota((CAP, 128), 0) >> 3), jnp.broadcast_to(logit_col, (CAP, 128)), 0.0)
    spread = spread.astype(BF16)
    fill = jnp.zeros((32, HD), BF16)

    counted = cnt.at[pl.ds(0, SEQ - 1)]
    remote(counted, counted, send_sem.at[0], recv_sem.at[0], sibling).wait_recv()
    counts = jnp.sum(cnt[...], axis=1)
    start = jnp.sum(jnp.where(iota((SEQ, 128), 0) < me, counts, 0), axis=0, keepdims=True)
    start_ref[...] = start

    n_half = iota((WPH * 8, CAP), 0)
    turn_half = ((n_half >> 3) - start[:, :CAP]) & 7
    pick_half = onehot(iota((WPH * 8, CAP), 1) == 8 * (n_half & 7) + turn_half)
    n_out = iota((WPH * MSG, 128), 0)
    t_out = n_out & 15
    turn = ((n_out >> 4) - start) & 7
    src = iota((WPH * MSG, 128), 1)
    b_from = jnp.where(t_out < 8, 8 * t_out + turn, jnp.where(t_out < 12, CAP + 4 * (n_out >> 4) + t_out - 8, -1))
    pick_b = onehot(src == b_from)
    src64 = iota((WPH * MSG, CAP), 1)
    pick_logit = onehot((t_out[:, :CAP] == 12) & ((src64 & 7) == turn[:, :CAP]))

    def send_rows(msg, rows, sem, recv):
        def send_one(n, carry):
            w = lax.rem(n + me, workers)
            dst = place_of(lax.div(w, WPH), lax.rem(w, WPH))

            @pl.when(dst != me)
            def _():
                remote(msg.at[w], rows.at[me], send_sem.at[sem], recv_sem.at[recv], {"seq": dst}).start()

            return carry

        lax.fori_loop(0, workers, send_one, 0, unroll=6)

    for ref, msg, rows, sem, recv in ((k_ref, msg_k, rows_k, 1, 1), (v_ref, msg_v, rows_v, 16, 8)):
        turned = dot(pick_half, ref[...]).astype(BF16)
        for k in range(heads):
            msg[pl.ds(k * WPH, WPH)] = turned[:, k * HD : (k + 1) * HD].reshape(WPH, 8, HD)
        send_rows(msg, rows, sem, recv)
    logit_rows = dot(pick_logit, spread)
    for k in range(heads):
        cols = slice(k * HD, (k + 1) * HD)
        both = dot(pick_b, jnp.concatenate([q_ref[:, cols], d_ref[:, cols], fill], axis=0)) + logit_rows
        msg_b[pl.ds(k * WPH, WPH)] = both.astype(BF16).reshape(WPH, MSG, HD)
    send_rows(msg_b, rows_b, 2, 2)
    left = []

    def gone(src, sem):
        left.append((src, sem))

    def done():
        for src, sem in left:
            remote(src, src, send_sem.at[sem], recv_sem.at[0], sibling).wait_send()

    def came(ref, sem):
        remote(ref, ref, send_sem.at[0], sem, sibling).wait_recv()

    @pl.when(is_worker)
    def _():
        own_k = pltpu.make_async_copy(msg_k.at[slot], rows_k.at[me], loc_sem.at[0])
        own_k.start()
        own_v = pltpu.make_async_copy(msg_v.at[slot], rows_v.at[me], loc_sem.at[3])
        own_v.start()
        own_b = pltpu.make_async_copy(msg_b.at[slot], rows_b.at[me], loc_sem.at[1])
        own_b.start()
        gone(msg_k.at[pl.ds(0, workers - 1)], 1)
        gone(msg_v.at[pl.ds(0, workers - 1)], 16)
        gone(msg_b.at[pl.ds(0, workers - 1)], 2)

        def peer(n, flip):
            return lax.rem(x + n, 4) * 2 + (1 - core if flip else core)

        def send_all(ref, sems, sem):
            remote(ref.at[cls], ref.at[cls], send_sem.at[sem], sems.at[cls], sibling).start()
            for n in (1, 3, 2):
                dst = {"seq": place_of(head, peer(n, 0))}
                remote(ref.at[cls], ref.at[cls], send_sem.at[sem], sems.at[cls], dst).start()
            gone(ref.at[pl.ds(0, 4)], sem)

        def pass_on(ref, sems, sem, n):
            block = ref.at[peer(n, 0)]
            came(block, sems.at[peer(n, 0)])
            remote(block, block, send_sem.at[sem], sems.at[peer(n, 0)], sibling).start()

        n_row = iota((SEQ, SEQ * MSG), 1)
        below = jnp.concatenate([counts] * 8, axis=1)
        at_h = iota((SEQ, SEQ * MSG), 0)
        start_n = jnp.sum(jnp.where(at_h < (n_row >> 4), below, 0), axis=0, keepdims=True)
        end_n = jnp.sum(jnp.where(at_h <= (n_row >> 4), below, 0), axis=0, keepdims=True)
        t_n = iota((1, SEQ * MSG), 1) & 15
        p_n = ((start_n - cls + 7) >> 3) + (t_n & 7)
        live_n = p_n < ((end_n - cls + 7) >> 3)
        lo_at = jnp.where(live_n & (t_n < 8), p_n, -1)
        p_sub = iota((CLS, SEQ * MSG), 0)
        take_lo = onehot(p_sub == lo_at)

        n_eight = iota((SEQ, SEQ * 8), 1)
        start_e = jnp.sum(jnp.where(at_h[:, : SEQ * 8] < (n_eight >> 3), below[:, : SEQ * 8], 0), axis=0, keepdims=True)
        end_e = jnp.sum(jnp.where(at_h[:, : SEQ * 8] <= (n_eight >> 3), below[:, : SEQ * 8], 0), axis=0, keepdims=True)
        p_e = ((start_e - cls + 7) >> 3) + (n_eight[0:1] & 7)
        e_at = jnp.where(p_e < ((end_e - cls + 7) >> 3), p_e, -1)
        take_eight = onehot(p_sub[:, : SEQ * 8] == e_at)

        came(rows_k.at[pl.ds(0, SEQ - 1)], recv_sem.at[1])
        own_k.wait()
        k_all[cls] = dot(take_eight, rows_k[...].reshape(SEQ * 8, HD)).astype(BF16)
        send_all(k_all, k_sem, 3)
        came(rows_v.at[pl.ds(0, SEQ - 1)], recv_sem.at[8])
        own_v.wait()
        v_all[cls] = dot(take_eight, rows_v[...].reshape(SEQ * 8, HD)).astype(BF16)
        send_all(v_all, v_sem, 4)

        m_sub = iota((CLS, SEQ), 0)
        residue_m = 8 * (m_sub & 7) + (m_sub >> 5)
        perm = jnp.broadcast_to(perm_ref[...], (CLS, SEQ))
        owner_m = jnp.sum(jnp.where(iota((CLS, SEQ), 1) == residue_m, perm, 0), axis=1, keepdims=True)
        d_at = MSG * owner_m + 8 + ((iota((CLS, 1), 0) & 31) >> 3)
        take_d = onehot(iota((CLS, SEQ * MSG), 1) == d_at)
        take_l = onehot(n_row == MSG * at_h + 12)
        tri = onehot(iota((SEQ, SEQ), 1) < iota((SEQ, SEQ), 0))
        starts = dot(tri, counts.astype(BF16)).astype(I32)
        base = (starts - cls + 7) >> 3
        after = (starts + counts - cls + 7) >> 3
        base2 = jnp.concatenate([base, base], axis=1)
        after2 = jnp.concatenate([after, after], axis=1)
        p_lane = iota((SEQ, CLS), 1)
        of_home = (base2 <= p_lane) & (p_lane < after2)
        lane_p = jnp.sum(jnp.where(of_home, p_lane - base2, 0), axis=0, keepdims=True)
        lanes = onehot(iota((128, CLS), 0) == lane_p)

        n_sub = iota((SEQ * MSG, SEQ), 0)
        rep = onehot((n_sub >> 4) == iota((SEQ * MSG, SEQ), 1))
        perm_o = jnp.broadcast_to(perm_ref[...], (SEQ, SEQ))
        res_o = jnp.sum(jnp.where(perm_o == iota((SEQ, SEQ), 0), iota((SEQ, SEQ), 1), 0), axis=1, keepdims=True)
        three = jnp.concatenate([base, after, jnp.broadcast_to(res_o, (SEQ, 128))], axis=1).astype(F32).astype(BF16)
        wide = dot(rep, three[:, :256]).astype(I32)
        t_col = iota((SEQ * MSG, 128), 0) & 15
        p_col = wide[:, :128] + (t_col & 7)
        live_col = p_col < wide[:, 128:256]
        lo_to = jnp.where(live_col & (t_col < 8), p_col, -1)
        hi_to = jnp.where(live_col & (t_col >= 8), p_col, -1)
        p_at = iota((SEQ * MSG, CLS), 1)
        put[0] = onehot(p_at == jnp.concatenate([lo_to, lo_to], axis=1))
        put[1] = onehot(p_at == jnp.concatenate([hi_to, hi_to], axis=1))
        rep_e = onehot((iota((SEQ * 8, SEQ), 0) >> 3) == iota((SEQ * 8, SEQ), 1))
        wide_e = dot(rep_e, three).astype(I32)
        t_e = iota((SEQ * 8, 128), 0) & 7
        e_col = wide_e[:, :128] + t_e
        e_to = jnp.where(e_col < wide_e[:, 128:256], e_col, -1)
        res_e = wide_e[:, 256:]
        o_to = jnp.where(t_e < 4, 32 * (res_e & 7) + 8 * t_e + (res_e >> 3), -1)
        put_e[0] = onehot(p_at[: SEQ * 8] == jnp.concatenate([e_to, e_to], axis=1))
        put_e[1] = onehot(p_at[: SEQ * 8] == jnp.concatenate([o_to, o_to], axis=1))
        put_g = onehot(iota((SEQ * 8, SEQ), 0) == 8 * iota((SEQ * 8, SEQ), 1) + 4)

        came(rows_b.at[pl.ds(0, SEQ - 1)], recv_sem.at[2])
        own_b.wait()
        b_rows = rows_b[...].reshape(SEQ * MSG, HD)
        dsend[...] = dot(take_d, b_rows).astype(BF16).reshape(WPH, 32, HD)

        def send_d(n, carry):
            to = lax.rem(cls + n, WPH)
            remote(dsend.at[to], dcls.at[cls], send_sem.at[6], recv_sem.at[3], {"seq": place_of(head, to)}).start()
            return carry

        lax.fori_loop(1, WPH, send_d, 0)
        dcls[cls] = dsend[cls]
        gone(dsend.at[pl.ds(0, WPH - 1)], 6)
        q = dot(take_lo, b_rows).astype(BF16)
        for n in (1, 3):
            pass_on(k_all, k_sem, 5, n)
        logit_h = dot(take_l, b_rows).astype(BF16)
        logit_p = jnp.sum(jnp.where(of_home, dot(logit_h, lanes), 0.0), axis=0, keepdims=True)
        gate = 1.0 / (1.0 + jnp.exp(-logit_p))

        top = jnp.full((1, CLS), -jnp.inf, F32)
        ahead = iota((CLS, CLS), 1) - iota((CLS, CLS), 0)
        order = ((0, 0), (0, 1), (1, 0), (3, 0), (1, 1), (3, 1), (2, 0), (2, 1))
        for n, flip in order:
            other = peer(n, flip)
            if (n, flip) == (1, 0):
                pass_on(k_all, k_sem, 5, 2)
            if flip:
                came(k_all.at[other], k_sem.at[other])
            later = jnp.where(other > cls, 1, 0)
            s = jnp.where(ahead >= later, dot_nt(k_all[other], q), -1e30)
            sbuf[2 * n + flip] = s
            top = jnp.maximum(top, jnp.max(s, axis=0, keepdims=True))
        gone(k_all.at[pl.ds(0, 3)], 5)
        for n in (1, 3):
            pass_on(v_all, v_sem, 7, n)
        total = jnp.zeros((1, CLS), F32)
        for n in range(WPH):
            e = jnp.exp2((sbuf[n] - top) * SCALE_LOG2)
            pbuf[n] = e.astype(BF16)
            total = total + jnp.sum(e, axis=0, keepdims=True)
        inv = 1.0 / total

        came(dcls.at[pl.ds(0, WPH - 1)], recv_sem.at[3])
        dy_t = dcls[...].reshape(CLS, HD).astype(F32).T
        dor_t = (dy_t * gate).astype(BF16).astype(F32)
        dor = (dor_t * inv).T.astype(BF16)

        def to_sibling(grads, part, pre, sems, sem, n):
            part[2 * n + 1] = grads.astype(BF16)
            remote(part.at[2 * n + 1], pre.at[n], send_sem.at[sem], sems.at[n], sibling).start()

        def to_class(grads, part, pre, pre_sems, total, sems, sem, n):
            came(pre.at[n], pre_sems.at[n])
            grads = grads + pre[n].astype(F32)
            if n:
                part[2 * n] = grads.astype(BF16)
                dst = {"seq": place_of(head, peer(n, 0))}
                remote(part.at[2 * n], total.at[x], send_sem.at[sem], sems.at[x], dst).start()
            return grads

        def collect(mine, total, sems):
            for n in (1, 3, 2):
                there = lax.rem(x + n, 4)
                came(total.at[there], sems.at[there])
                mine = mine + total[there].astype(F32)
            return mine.astype(BF16)

        far_first = (2, 1, 3, 0)
        for n in far_first:
            to_sibling(dot(pbuf[2 * n + 1], dor), part_v, pre_v, pre_v_sem, 9, n)
        gone(part_v.at[pl.ds(0, 4)], 9)
        pass_on(v_all, v_sem, 7, 2)
        for n in far_first:
            mine_v = to_class(dot(pbuf[2 * n], dor), part_v, pre_v, pre_v_sem, sum_v, sum_v_sem, 10, n)
        gone(part_v.at[pl.ds(0, 3)], 10)
        gone(v_all.at[pl.ds(0, 3)], 7)
        out_t = jnp.zeros((HD, CLS), F32)
        for n, flip in order:
            other = peer(n, flip)
            if flip:
                came(v_all.at[other], v_sem.at[other])
            out_t = out_t + dot_tn(v_all[other], pbuf[2 * n + flip])
        out_t = out_t * inv
        delta = jnp.sum(dor_t * out_t, axis=0, keepdims=True) * inv
        gate_grad = jnp.sum(dy_t * out_t, axis=0, keepdims=True)
        gsend[...] = (out_t * gate).T.astype(BF16).reshape(WPH, 32, HD)

        def send_gated(n, carry):
            to = lax.rem(cls + n, WPH)
            remote(gsend.at[to], gchk.at[cls], send_sem.at[8], recv_sem.at[4], {"seq": place_of(head, to)}).start()
            return carry

        lax.fori_loop(1, WPH, send_gated, 0)
        gchk[cls] = gsend[cls]
        gone(gsend.at[pl.ds(0, WPH - 1)], 8)
        dq_t = jnp.zeros((HD, CLS), F32)
        for flip in (1, 0):
            for n in far_first:
                other = peer(n, flip)
                dp = dot_nt(v_all[other], dor)
                ds = (pbuf[2 * n + flip].astype(F32) * (dp - delta)).astype(BF16)
                dq_t = dq_t + dot_tn(k_all[other], ds)
                if flip:
                    to_sibling(dot(ds, q) * SCALE, part_k, pre_k, pre_k_sem, 11, n)
                else:
                    pbuf[2 * n] = ds
        for n in far_first:
            mine_k = to_class(dot(pbuf[2 * n], q) * SCALE, part_k, pre_k, pre_k_sem, sum_k, sum_k_sem, 12, n)
        gone(part_k.at[pl.ds(0, 4)], 11)
        gone(part_k.at[pl.ds(0, 3)], 12)

        def send_back(back, home, sem, recv, own):
            def send_one(n, carry):
                to = lax.rem(me + n, SEQ)
                remote(back.at[to], home.at[slot], send_sem.at[sem], recv_sem.at[recv], {"seq": to}).start()
                return carry

            lax.fori_loop(1, SEQ, send_one, 0, unroll=7)
            gone(back.at[pl.ds(0, SEQ - 1)], sem)
            mine = pltpu.make_async_copy(back.at[me], home.at[slot], loc_sem.at[own])
            mine.start()
            return mine

        dqc = (dq_t * SCALE).T.astype(BF16)
        back_q[...] = dot(put_e[0], dqc).astype(BF16).reshape(SEQ, 8, HD)
        own_q = send_back(back_q, home_q, 14, 6, 1)
        gg_home = dot_nt(jnp.where(of_home, gate_grad, 0.0).astype(BF16), lanes).astype(BF16)
        came(gchk.at[pl.ds(0, WPH - 1)], recv_sem.at[4])
        full = dot(put_g, gg_home) + dot(put_e[1], gchk[...].reshape(CLS, HD))
        back_c[...] = full.astype(BF16).reshape(SEQ, 8, HD)
        own_c = send_back(back_c, home_c, 17, 9, 3)
        rest = dot(put[1], collect(mine_v, sum_v, sum_v_sem))
        full = dot(put[0], collect(mine_k, sum_k, sum_k_sem)) + rest
        back_b[...] = full.astype(BF16).reshape(SEQ, MSG, HD)
        own_b = send_back(back_b, home_b, 15, 7, 0)
        own_q.wait()
        own_c.wait()
        own_b.wait()
        came(home_c.at[pl.ds(0, workers - 1)], recv_sem.at[9])

    @pl.when(jnp.logical_not(is_worker))
    def _():
        came(home_c, recv_sem.at[9])

    keep_c = pltpu.make_async_copy(home_c, home_c_out, loc_sem.at[2])
    keep_c.start()
    gate_rows = jnp.zeros((CAP, HD), F32)
    take_g = onehot((iota((CAP, 128), 1) == 8 * ((start + iota((CAP, 128), 0)) & 7) + 4)[:, :CAP])
    for k in range(heads):
        gate_rows = gate_rows + dot(take_g, home_c[pl.ds(k * WPH, WPH)].reshape(WPH * 8, HD))
    mine_lane = iota((CAP, HD), 1) == (iota((CAP, HD), 0) >> 3)
    gate_grad = jnp.sum(jnp.where(mine_lane, gate_rows, 0.0), axis=1, keepdims=True)
    gg[tp] = jnp.broadcast_to(gate_grad, (CAP, 128))
    for n in range(1, n_tp):
        remote(gg.at[tp], gg.at[tp], send_sem.at[13], recv_sem.at[5], {"tp": lax.rem(tp + n, n_tp)}).start()

    if n_tp > 1:
        others = gg.at[pl.ds(0, n_tp - 1)]
        remote(others, others, send_sem.at[13], recv_sem.at[5], sibling).wait()
    gate_col = 1.0 / (1.0 + jnp.exp(-logit_col))
    logit_grad = jnp.sum(gg[...], axis=0)[:, 0:1] * gate_col * (1.0 - gate_col)
    router = jnp.sum(jnp.where(spots, jnp.broadcast_to(logit_grad, (CAP, TOK)), 0.0), axis=0, keepdims=True)
    row_ref[...] = router

    @pl.when(is_worker)
    def _():
        done()
        came(home_q.at[pl.ds(0, workers - 1)], recv_sem.at[6])
        came(home_b.at[pl.ds(0, workers - 1)], recv_sem.at[7])

    @pl.when(jnp.logical_not(is_worker))
    def _():
        remote(msg_k, msg_k, send_sem.at[1], recv_sem.at[1], sibling).wait_send()
        remote(msg_v, msg_v, send_sem.at[16], recv_sem.at[8], sibling).wait_send()
        remote(msg_b, msg_b, send_sem.at[2], recv_sem.at[2], sibling).wait_send()
        came(home_q, recv_sem.at[6])
        came(home_b, recv_sem.at[7])

    keep_c.wait()
    remote(counted, counted, send_sem.at[0], recv_sem.at[0], sibling).wait_send()


def finish(heads, start_ref, row_ref, home_c, home_q, home_b, gated_ref, dq_ref, dk_ref, dv_ref, router_ref):
    start = start_ref[...]
    router_ref[...] = row_ref[...]
    col = iota((CAP, 128), 1)
    j = iota((CAP, 128), 0)
    from_cls = MSG * ((start + j) & 7)
    lo = from_cls + (j >> 3)
    take_lo = col == lo
    take_e = onehot((col == 8 * ((start + j) & 7) + (j >> 3))[:, :CAP])
    take_o = onehot(((col == 8 * (j >> 2) + (j & 3)) & (j < 32))[:32, :CAP])
    take_b = jnp.concatenate([onehot(take_lo), onehot(col == lo + 8)], axis=0)
    for k in range(heads):
        cols = slice(k * HD, (k + 1) * HD)
        dq_ref[:, cols] = dot(take_e, home_q[pl.ds(k * WPH, WPH)].reshape(WPH * 8, HD)).astype(BF16)
        gated_ref[:, cols] = dot(take_o, home_c[pl.ds(k * WPH, WPH)].reshape(WPH * 8, HD)).astype(BF16)
        res = dot(take_b, home_b[pl.ds(k * WPH, WPH)].reshape(WPH * MSG, HD))
        dk_ref[:, cols] = res[0:64].astype(BF16)
        dv_ref[:, cols] = res[64:128].astype(BF16)


def body(picked, owner_perm, router_logit, queries, keys, values, out_grad):
    n_tp = lax.axis_size("tp")
    heads = queries.shape[1] // HD
    width = heads * HD
    workers = heads * WPH
    picks = out_grad.shape[0]
    vmem = pl.BlockSpec(memory_space=pltpu.VMEM)
    hbm = pl.BlockSpec(memory_space=pltpu.HBM)
    dma = pltpu.SemaphoreType.DMA
    picked = picked.reshape(1, CAP)
    router_logit = router_logit.reshape(2, TOK // 2)
    start, router, home_c, home_q, home_b = pl.pallas_call(
        functools.partial(kernel, n_tp, heads),
        out_shape=(
            jax.ShapeDtypeStruct((1, 128), I32),
            jax.ShapeDtypeStruct((1, TOK), F32),
            jax.ShapeDtypeStruct((workers, 8, HD), BF16),
            jax.ShapeDtypeStruct((workers, 8, HD), BF16),
            jax.ShapeDtypeStruct((workers, MSG, HD), BF16),
        ),
        in_specs=[hbm] * 7,
        out_specs=[vmem, vmem, hbm, hbm, hbm],
        scratch_shapes=[
            pltpu.VMEM((1, CAP), I32),
            pltpu.VMEM((1, SEQ), I32),
            pltpu.VMEM((2, TOK // 2), BF16),
            pltpu.VMEM((CAP, width), BF16),
            pltpu.VMEM((CAP, width), BF16),
            pltpu.VMEM((CAP, width), BF16),
            pltpu.VMEM((picks, width), BF16),
            pltpu.VMEM((1, 128), I32),
            pltpu.VMEM((SEQ, 1, 128), I32),
            pltpu.VMEM((workers, 8, HD), BF16),
            pltpu.VMEM((workers, 8, HD), BF16),
            pltpu.VMEM((workers, MSG, HD), BF16),
            pltpu.VMEM((SEQ, 8, HD), BF16),
            pltpu.VMEM((SEQ, 8, HD), BF16),
            pltpu.VMEM((SEQ, MSG, HD), BF16),
            pltpu.VMEM((WPH, CLS, HD), BF16),
            pltpu.VMEM((WPH, CLS, HD), BF16),
            pltpu.VMEM((WPH, 32, HD), BF16),
            pltpu.VMEM((WPH, 32, HD), BF16),
            pltpu.VMEM((2, SEQ * MSG, CLS), BF16),
            pltpu.VMEM((2, SEQ * 8, CLS), BF16),
            pltpu.VMEM((WPH, CLS, CLS), F32),
            pltpu.VMEM((WPH, CLS, CLS), BF16),
            pltpu.VMEM((WPH, CLS, HD), BF16),
            pltpu.VMEM((WPH, CLS, HD), BF16),
            pltpu.VMEM((4, CLS, HD), BF16),
            pltpu.VMEM((4, CLS, HD), BF16),
            pltpu.VMEM((4, CLS, HD), BF16),
            pltpu.VMEM((4, CLS, HD), BF16),
            pltpu.VMEM((WPH, 32, HD), BF16),
            pltpu.VMEM((WPH, 32, HD), BF16),
            pltpu.VMEM((n_tp, CAP, 128), F32),
            pltpu.VMEM((SEQ, 8, HD), BF16),
            pltpu.VMEM((SEQ, 8, HD), BF16),
            pltpu.VMEM((SEQ, MSG, HD), BF16),
            pltpu.VMEM((workers, 8, HD), BF16),
            dma((7,)),
            dma((18,)),
            dma((10,)),
            dma((WPH,)),
            dma((WPH,)),
            dma((4,)),
            dma((4,)),
            dma((4,)),
            dma((4,)),
            dma((4,)),
        ],
        compiler_params=pltpu.CompilerParams(
            collective_id=0, has_side_effects=True, vmem_limit_bytes=60 * 1024 * 1024
        ),
    )(
        picked,
        owner_perm.reshape(1, SEQ),
        router_logit,
        queries,
        keys,
        values,
        out_grad,
    )
    gated, dq, dk, dv, router = pl.pallas_call(
        functools.partial(finish, heads),
        out_shape=(
            jax.ShapeDtypeStruct((picks, width), BF16),
            jax.ShapeDtypeStruct((CAP, width), BF16),
            jax.ShapeDtypeStruct((CAP, width), BF16),
            jax.ShapeDtypeStruct((CAP, width), BF16),
            jax.ShapeDtypeStruct((1, TOK), F32),
        ),
        in_specs=[vmem] * 5,
        out_specs=[vmem] * 5,
        compiler_params=pltpu.CompilerParams(vmem_limit_bytes=60 * 1024 * 1024),
    )(start, router, home_c, home_q, home_b)
    return gated, dq, dk, dv, router.reshape(TOK)


def solution(mesh):
    return jax.shard_map(
        body,
        mesh=mesh,
        in_specs=(P("seq"), P(), P("seq"), P("seq", "tp"), P("seq", "tp"), P("seq", "tp"), P("seq", "tp")),
        out_specs=(P("seq", "tp"), P("seq", "tp"), P("seq", "tp"), P("seq", "tp"), P("seq")),
        check_vma=False,
    )
```
